32 devices in a mesh: dp: 16 (over z, y, x), blk: 2 (over core).
Axes of the slice: x: 2, y: 2, z: 4, core: 2. Of those that a mesh axis runs over, the one named last changes fastest.
Arguments:
- tokens: bfloat16 [16, 1024, 768], P('dp', 'blk'), may hold values from -6 to 6
- lengths: int32 [16], P('dp'), may hold values from 1 to 1024, as said below
- cotangent: bfloat16 [16, 1024, 768], P('dp', 'blk'), may hold values from -6 to 6
- query_weight: bfloat16 [768, 768], replicated, may hold values from -0.3125 to 0.3125
- query_bias: float32 [768], replicated, may hold values from -3 to 3
- key_matrix: bfloat16 [768, 768], replicated, may hold values from -0.3125 to 0.3125
- value_weight: bfloat16 [768, 768], replicated, may hold values from -0.21875 to 0.21875
- value_bias: float32 [768], replicated, may hold values from -1.75 to 1.75
- output_weight: bfloat16 [768, 768], replicated, may hold values from -1.75 to 1.75
- output_bias: float32 [768], replicated, may hold values from -1.75 to 1.75
- attn_gain: float32 [768], replicated, may hold values from 0.5 to 1.5
- attn_shift: float32 [768], replicated, may hold values from -1.75 to 1.75
- up_weight: bfloat16 [768, 3072], replicated, may hold values from -0.21875 to 0.21875
- up_bias: float32 [3072], replicated, may hold values from -3 to 3
- down_weight: bfloat16 [3072, 768], replicated, may hold values from -0.15625 to 0.15625
- down_bias: float32 [768], replicated, may hold values from -1.75 to 1.75
- ffn_gain: float32 [768], replicated, may hold values from 0.5 to 1.5
- ffn_shift: float32 [768], replicated, may hold values from -1.75 to 1.75
Outputs:
- encoded: bfloat16 [16, 1024, 768], P('dp', 'blk')
- token_grad: bfloat16 [16, 1024, 768], P('dp', 'blk')
- qweight_grad: float32 [768, 768], P('dp')
- qbias_grad: float32 [768], replicated
- kweight_grad: float32 [768, 768], P('dp')
- vweight_grad: float32 [768, 768], P('dp')
- vbias_grad: float32 [768], replicated
- oweight_grad: float32 [768, 768], P('dp')
- obias_grad: float32 [768], replicated
- again_grad: float32 [768], replicated
- ashift_grad: float32 [768], replicated
- uweight_grad: float32 [768, 3072], P('dp')
- ubias_grad: float32 [3072], replicated
- dweight_grad: float32 [3072, 768], P('dp')
- dbias_grad: float32 [768], replicated
- fgain_grad: float32 [768], replicated
- fshift_grad: float32 [768], replicated
The draws below stay inside these ranges and needn't reach their ends.
Inputs may be any that keep to these rules, and one draw needn't show every extreme that they name: `lengths`: among the 1 sequence of each index of dp, one has all 1024 positions valid.
All inputs are finite; a program needn't handle non-finite values.
Results may differ from the reference program's by a relative error of at most 0.02.
Values may be sent and summed in bfloat16 or wider, within the bound.
A program may use at most 128 MiB of HBM per device.

```python
import math
import jax
import jax.numpy as jnp
from jax import lax

D = 768
HEADS = 12
HD = 64
FF = 3072
SEQS = 1
SEQ = 1024
SEQS_ALL = 16


def draw_lengths(key, part):
    key = jax.random.fold_in(key, 7)
    first, second = jax.random.split(key)
    groups = SEQS_ALL // SEQS
    raw_lengths = jax.random.randint(first, (groups, SEQS), 1, SEQ + 1, dtype=jnp.int32)
    chosen = jax.random.randint(second, (groups, 1), 0, SEQS, dtype=jnp.int32)
    slots = jnp.arange(SEQS, dtype=jnp.int32)[None, :]
    return jnp.where(slots == chosen, SEQ, raw_lengths).astype(jnp.int32).reshape(SEQS_ALL)


def with_spikes(values, key, source, target, parts, factor):
    def block_of(position):
        return (jnp.arange(values.shape[position]) // (values.shape[position] // parts)).reshape((-1,) + (1,) * (values.ndim - 1 - position))

    first = jax.random.permutation(key, parts)[block_of(target)]
    other_side = (block_of(target) + parts // 2) % parts
    return jnp.where((block_of(source) == first) | (block_of(source) == other_side), factor * values, values)


def steps_of(key, extent, pieces, low, high):
    gain, own = 1.0, jax.random.fold_in(key, 6)
    for dim, blocks in pieces:
        steps = jnp.exp(jax.random.uniform(jax.random.fold_in(own, dim), (blocks,), jnp.float32, low / len(pieces), high / len(pieces)))
        gain = gain * jnp.repeat(steps, extent[dim] // blocks).reshape([-1 if axis == dim else 1 for axis in range(len(extent))])
    return gain


def noise(own_key, dims, width, reach, cuts=(), kind=jnp.bfloat16):
    gain = steps_of(own_key, dims, cuts, -0.22, 0.18) if cuts else 1.0
    entries = jax.random.normal(own_key, dims, jnp.float32) * width * gain
    return jnp.minimum(jnp.maximum(entries, -reach), reach).astype(kind)


def gaussian_with(key, dims, scale, most, cuts, heavy, kind=jnp.bfloat16):
    values = scale * jax.random.normal(key, dims, jnp.float32)
    if cuts:
        values = values * steps_of(key, dims, cuts, -0.22, 0.18)
    return jnp.clip(with_spikes(values, jax.random.fold_in(key, 3), *heavy), -most, most).astype(kind)


def setup_inputs(seed: int = 0) -> dict:
    seeds = jax.random.split(jax.random.key(seed), 19)
    return {
        "tokens": gaussian_with(seeds[0], (SEQS_ALL, SEQ, D), 1.0, 6.0, ((0, 16), (1, 2)), (0, 2, 16, 2.0)),
        "lengths": draw_lengths(jax.random.fold_in(seeds[18], 71), 0),
        "cotangent": noise(seeds[2], (SEQS_ALL, SEQ, D), 1.0, 6.0, ((0, 16), (1, 2))),
        "query_weight": noise(seeds[3], (D, D), (D // 2) ** -0.5, 0.3125),
        "query_bias": noise(seeds[4], (D,), 0.5, 3.0, (), jnp.float32),
        "key_matrix": noise(seeds[5], (D, D), (D // 2) ** -0.5, 0.3125),
        "value_weight": noise(seeds[6], (D, D), D ** -0.5, 0.21875),
        "value_bias": noise(seeds[7], (D,), 0.3, 1.75, (), jnp.float32),
        "output_weight": noise(seeds[8], (D, D), (max(D // 64, 4)) ** -0.5, 1.75),
        "output_bias": noise(seeds[9], (D,), 0.3, 1.75, (), jnp.float32),
        "attn_gain": jnp.clip(1.0 + 0.1 * jax.random.normal(seeds[10], (D,), jnp.float32), 0.5, 1.5),
        "attn_shift": noise(seeds[11], (D,), 0.3, 1.75, (), jnp.float32),
        "up_weight": noise(seeds[12], (D, FF), D ** -0.5, 0.21875),
        "up_bias": noise(seeds[13], (FF,), 0.5, 3.0, (), jnp.float32),
        "down_weight": noise(seeds[14], (FF, D), (FF // 2) ** -0.5, 0.15625),
        "down_bias": noise(seeds[15], (D,), 0.3, 1.75, (), jnp.float32),
        "ffn_gain": jnp.clip(1.0 + 0.1 * jax.random.normal(seeds[16], (D,), jnp.float32), 0.5, 1.5),
        "ffn_shift": noise(seeds[17], (D,), 0.3, 1.75, (), jnp.float32),
    }


@jax.custom_vjp
def low(v):
    return lax.optimization_barrier(v.astype(jnp.bfloat16)).astype(jnp.float32)

@jax.custom_vjp
def low_back(v):
    return v

def low_keep(v):
    return (low(v), None)

def low_pass(kept, grad):
    return (grad,)

def back_keep(v):
    return (v, None)

def back_low(kept, grad):
    return (low(grad),)
low.defvjp(low_keep, low_pass)
low_back.defvjp(back_keep, back_low)
EPSILON = 1e-05
PRECISE = lax.Precision.HIGHEST

def norm_rows(values_in, gain_vec, shift_vec):
    row_mean = lax.optimization_barrier(jnp.mean(values_in, axis=-1, keepdims=True))
    centred = values_in - row_mean
    spread = lax.optimization_barrier(jnp.mean(centred * centred, axis=-1, keepdims=True))
    return centred * lax.rsqrt(spread + EPSILON) * gain_vec + shift_vec

def gelu_exact(values_in):
    return 0.5 * values_in * (1.0 + lax.erf(values_in * (1.0 / math.sqrt(2.0))))

def project(left, right):
    return jnp.dot(left, right, precision=PRECISE)

def encoder_layer(tokens, seq_length, params):
    query_weight, query_bias, key_matrix, value_weight, value_bias, output_weight, output_bias, attn_gain, attn_shift, up_weight, up_bias, down_weight, down_bias, ffn_gain, ffn_shift = params
    score_scale = 1.0 / math.sqrt(HD)
    queries = low(low_back(project(tokens, query_weight) + query_bias))
    keyset = low(low_back(project(tokens, key_matrix)))
    valset = low(low_back(project(tokens, value_weight) + value_bias))
    split_shape = (SEQ, HEADS, HD)
    scores = jnp.einsum('qhd,khd->hqk', queries.reshape(split_shape), keyset.reshape(split_shape), precision=PRECISE)
    scores = low_back(scores * score_scale)
    counted = jnp.arange(SEQ, dtype=jnp.int32) < seq_length
    masked = jnp.where(counted[None, None, :], scores, -1e+30)
    largest = lax.optimization_barrier(jnp.max(masked, axis=-1, keepdims=True))
    raised = jnp.exp(masked - largest)
    soft_probs = raised / lax.optimization_barrier(jnp.sum(raised, axis=-1, keepdims=True))
    mixed_out = jnp.einsum('hqk,khd->qhd', low(soft_probs), valset.reshape(split_shape), precision=PRECISE)
    mixed_out = low(low_back(mixed_out.reshape(SEQ, HEADS * HD)))
    attended = low_back(project(mixed_out, output_weight) + output_bias)
    hidden = norm_rows(tokens + attended, attn_gain, attn_shift)
    inner_act = low_back(project(low(hidden), up_weight) + up_bias)
    active = low(gelu_exact(inner_act))
    ffn_out = low_back(project(active, down_weight) + down_bias)
    return norm_rows(hidden + ffn_out, ffn_gain, ffn_shift)

def reference(tokens, lengths, cotangent, query_weight, query_bias, key_matrix, value_weight, value_bias, output_weight, output_bias, attn_gain, attn_shift, up_weight, up_bias, down_weight, down_bias, ffn_gain, ffn_shift):
    params = tuple((weight.astype(jnp.float32) for weight in (query_weight, query_bias, key_matrix, value_weight, value_bias, output_weight, output_bias, attn_gain, attn_shift, up_weight, up_bias, down_weight, down_bias, ffn_gain, ffn_shift)))

    def one_sequence(totals, item):
        seq_tokens, seq_length, seq_cot = item
        encoded, pull = jax.vjp(lambda activations, weights: encoder_layer(activations, seq_length, weights), seq_tokens.astype(jnp.float32), params)
        grad_tokens, grad_weights = pull(seq_cot.astype(jnp.float32))
        totals = jax.tree.map(jnp.add, totals, grad_weights)
        return (totals, (encoded.astype(jnp.bfloat16), grad_tokens.astype(jnp.bfloat16)))
    start = tuple((jnp.zeros_like(weight) for weight in params))
    totals, (encoded, token_grad) = lax.scan(one_sequence, start, (tokens, lengths, cotangent))
    return (encoded, token_grad, totals[0], totals[1], totals[2], totals[3], totals[4], totals[5], totals[6], totals[7], totals[8], totals[9], totals[10], totals[11], totals[12], totals[13], totals[14])
```

```python
import math

import jax
import jax.numpy as jnp
from jax import lax
from jax.experimental import pallas as pl
from jax.experimental.pallas import tpu as pltpu
from jax.sharding import PartitionSpec as P

MESH = pl.DeviceIdType.MESH
f32, bf16 = jnp.float32, jnp.bfloat16

HEADS = 12
EPSILON = 1e-05

LOG2E = math.log2(math.e)
LN2 = math.log(2.0)
AX = {"zh": (3, 1), "zl": (2, 2), "y": (1, 3), "x": (0, 4)}
BITS = ("c", "x", "y", "zl", "zh")
ORDERS = (("x", "y", "zl", "zh"), ("y", "x", "zl", "zh"), ("zl", "x", "y", "zh"), ("zl", "y", "x", "zh"))
PIECES = (
    ("D0", 96, 256, 0), ("D1", 96, 256, 1), ("D2", 96, 256, 2),
    ("U0", 96, 256, 0), ("U1", 96, 256, 1), ("U2", 96, 256, 3),
    ("O0", 48, 128, 0), ("O1", 48, 128, 1), ("O2", 48, 128, 2),
    ("Q", 48, 384, 0), ("K", 48, 384, 1), ("V", 48, 384, 3),
)
NAMES = [p[0] for p in PIECES]
N_PIECES = len(PIECES)
ROW_Q, ROW_V, ROW_O, ROW_AGAIN, ROW_ASHIFT, ROW_U, ROW_D, ROW_FGAIN, ROW_FSHIFT = 0, 1, 2, 3, 4, 5, 9, 10, 11


def bit(dp, ax):
    return lax.rem(lax.div(dp, 1 << AX[ax][0]), 2)


def peer_of(ax):
    dp, c = lax.axis_index("dp"), lax.axis_index("blk")
    if ax == "c":
        return (dp, 1 - c)
    return (dp + (1 - 2 * bit(dp, ax)) * (1 << AX[ax][0]), c)


def dot_nn(a, b):
    return jnp.dot(a, b, preferred_element_type=f32)


def dot_nt(a, b):
    return lax.dot_general(a, b, (((1,), (1,)), ((), ())), preferred_element_type=f32)


def dot_tn(a, b):
    return lax.dot_general(a, b, (((0,), (0,)), ((), ())), preferred_element_type=f32)


def fold8(v):
    return jnp.sum(v.reshape(v.shape[0] // 8, 8, v.shape[1]), axis=0)


class Piece:
    def __init__(self, idx, own, other, recvs, fin, ssem, rsem):
        self.name, self.R, self.C, order = PIECES[idx]
        self.idx, self.own, self.other, self.recvs, self.fin = idx, own, other, recvs, fin
        self.ssem, self.rsem = ssem, rsem
        self.order = ORDERS[order]
        self.dp = lax.axis_index("dp")
        self.cp, self.done = {}, set()

    def view(self, k, mine):
        idx = [slice(None)] * 4
        for j in range(k):
            ax = self.order[j]
            own = bit(self.dp, ax)
            idx[AX[ax][1] - 1] = own if (j < k - 1 or mine) else 1 - own
        return tuple(idx)

    def copy(self, k, src, dst, ax):
        cp = pltpu.make_async_remote_copy(
            src, dst, self.ssem.at[self.idx, k], self.rsem.at[self.idx, k], device_id=peer_of(ax), device_id_type=MESH
        )
        cp.start()
        self.cp[k] = cp

    def start(self):
        self.copy(0, self.other, self.recvs[0], "c")

    def finish(self, k):
        self.cp[k].wait_recv()
        v = self.view(k, True)
        total = self.own[v].astype(f32) + self.recvs[k][...].astype(f32)
        if k < 4:
            self.own[v] = total.astype(bf16)
            self.copy(k + 1, self.own.at[self.view(k + 1, False)], self.recvs[k + 1], self.order[k])
        else:
            self.fin[0][...] = total
            self.copy(5, self.fin[0], self.fin[1], "c")

    def sent(self, k):
        self.cp[k].wait_send()
        self.done.add(k)


def layer_kernel(*refs):
    (tok_h, len_s, cot_h, wq_h, bq, wk_h, wv_h, bv, wo_h, bo, g1, b1, wu_h, bu, wd_h, bd, g2, b2) = refs[:18]
    enc_o, tg_o, qg_o, kg_o, vg_o, og_o, ug_o, dg_o, vec_o, e_hbm = refs[18:28]
    (X, WS, WO, Q, KO, KP, VO, VP, MB, MIX, LINV, T1, T2, T3, RSTD, HL, G, DO, CD, FAB, KR, VR,
     DU, OB, QB, RDU, RO, RQ, SDU, SO, SQ, FDU, FO, FQ, b_acc, b_recv,
     wsem, esem, osem, ksem_s, ksem_r, ssem, rsem) = refs[28:]
    (R1DU, R2DU, R3DU, R4DU), (R1O, R2O, R3O, R4O), (R1Q, R2Q, R3Q, R4Q) = SDU, SO, SQ
    c = lax.axis_index("blk")
    rows = X.shape[0]
    D = X.shape[1]
    scale = 1.0 / math.sqrt(D // HEADS)

    def load(src, dst, sem):
        cp = pltpu.make_async_copy(src, dst, sem)
        cp.start()
        return cp

    ld_x = load(tok_h.at[0], X, wsem.at[5])
    ld_k = load(wk_h, WS.at[0], wsem.at[0])
    ld_v = load(wv_h, WS.at[1], wsem.at[1])
    ld_q = load(wq_h, WS.at[2], wsem.at[2])
    ld_o = load(wo_h, WO, wsem.at[4])
    ld_c = load(cot_h.at[0], CD, wsem.at[6])

    barrier = pltpu.get_barrier_semaphore()
    for ax in BITS:
        pl.semaphore_signal(barrier, inc=1, device_id=peer_of(ax), device_id_type=MESH)

    def pick(half, mine, theirs):
        return jnp.where(half == c, mine, theirs)

    pieces = {}
    for i, (name, _, _, _) in enumerate(PIECES):
        if name[0] in "DU":
            t = int(name[1])
            own, other, recvs, fin = DU.at[i], DU.at[6 + t], [r.at[i] for r in (RDU, R1DU, R2DU, R3DU, R4DU)], FDU.at[i]
        elif name[0] == "O":
            t = int(name[1])
            own, other, recvs, fin = OB.at[0, t], OB.at[1, t], [r.at[t] for r in (RO, R1O, R2O, R3O, R4O)], FO.at[t]
        else:
            t = "QKV".index(name)
            own, other, recvs, fin = QB.at[0, t], QB.at[1, t], [r.at[t] for r in (RQ, R1Q, R2Q, R3Q, R4Q)], FQ.at[t]
        pieces[name] = Piece(i, own, other, recvs, [fin.at[0], fin.at[1]], ssem, rsem)

    def step(*events):
        for name, k in events:
            pieces[name].finish(k)

    lane = lax.broadcasted_iota(jnp.int32, (rows, 128), 1)
    low = lane < 64
    length = len_s[0]
    pos = lax.broadcasted_iota(jnp.int32, (rows, 128), 0)
    MB[0] = jnp.where(pos + c * rows < length, 0.0, -1e30).astype(bf16)
    MB[1] = jnp.where(pos + (1 - c) * rows < length, 0.0, -1e30).astype(bf16)

    def kv_send(src, dst, i):
        cp = pltpu.make_async_remote_copy(
            src, dst, ksem_s.at[6, i], ksem_r.at[6, i], device_id=peer_of("c"), device_id_type=MESH
        )
        cp.start()
        return cp

    ld_x.wait()
    ld_k.wait()
    KO[...] = dot_nn(X[...], WS[0]).astype(bf16)
    pl.semaphore_wait(barrier, 5)
    send_k = kv_send(KO, KP, 0)
    ld_v.wait()
    VO[...] = (dot_nn(X[...], WS[1]) + bv[...]).astype(bf16)
    send_v = kv_send(VO, VP, 1)
    FFC = 512

    def load_ffn(n, j):
        a = 2 * (n % 2)
        return (
            load(wu_h.at[:, pl.ds(FFC * j, FFC)], WS.at[a, :, pl.ds(0, FFC)], wsem.at[a]),
            load(wd_h.at[pl.ds(FFC * j, FFC), :], WS.at[a + 1, pl.ds(0, FFC), :], wsem.at[a + 1]),
        )

    ffn_order = [0, 1, 2, 3, 4, 5, 0, 3, 1, 4, 2, 5]
    ffn_loads = {0: load_ffn(0, ffn_order[0])}
    ld_q.wait()
    Q[...] = ((dot_nn(X[...], WS[2]) + bq[...]) * (scale * LOG2E)).astype(bf16)
    ffn_loads[1] = load_ffn(1, ffn_order[1])
    send_k.wait_recv()
    send_v.wait_recv()

    one, zero = jnp.ones((rows, 128), bf16), jnp.zeros((rows, 128), bf16)
    hot = [jnp.where(lane == 64, 1.0, 0.0).astype(bf16), jnp.where(lane == 0, 1.0, 0.0).astype(bf16)]

    def own_lanes(j, mine, rest):
        return jnp.where(low, mine, rest) if j == 0 else jnp.where(low, rest, mine)

    e_out = {}
    for p in range(HEADS // 2):
        ls = slice(128 * p, 128 * p + 128)
        res = []
        for j in range(2):
            h = 2 * p + j
            q = own_lanes(j, Q[:, ls], hot[j])
            s_o = dot_nt(q, own_lanes(j, KO[:, ls], MB[0]))
            s_p = dot_nt(q, own_lanes(j, KP[:, ls], MB[1]))
            m = jnp.maximum(jnp.max(s_o, axis=1, keepdims=True), jnp.max(s_p, axis=1, keepdims=True))
            e_o = jnp.exp2(s_o - m).astype(bf16)
            e_p = jnp.exp2(s_p - m).astype(bf16)
            base = 1024 * (h % 6)
            if h >= 6:
                e_out.pop(h - 6).wait()
            FAB[base : base + 512, :] = e_o
            FAB[base + 512 : base + 1024, :] = e_p
            e_out[h] = load(FAB.at[pl.ds(base, 1024), :], e_hbm.at[h], esem.at[h % 6])
            res.append(dot_nn(e_o, own_lanes(j, VO[:, ls], one)) + dot_nn(e_p, own_lanes(j, VP[:, ls], one)))
        inv = 1.0 / pltpu.roll(jnp.where(low, res[1], res[0]), 64, 1)
        MIX[:, ls] = (jnp.where(low, res[0], res[1]) * inv).astype(bf16)
        LINV[:, ls] = inv

    ld_o.wait()
    T2[...] = dot_nn(MIX[...], WO[...])
    BR = 128
    for r in range(0, rows, BR):
        rs = slice(r, r + BR)
        r1 = X[rs, :].astype(f32) + (T2[rs, :] + bo[...])
        cen = r1 - jnp.mean(r1, axis=1, keepdims=True)
        rstd = lax.rsqrt(jnp.mean(cen * cen, axis=1, keepdims=True) + EPSILON)
        xh = cen * rstd
        T1[rs, :] = xh
        RSTD[rs, :] = rstd
        HL[rs, :] = (xh * g1[...] + b1[...]).astype(bf16)
    for h in sorted(e_out):
        e_out.pop(h).wait()

    for n in range(6):
        j = ffn_order[n]
        a = 2 * (n % 2)
        ffn_loads[n][0].wait()
        u = dot_nn(HL[...], WS[a, :, :FFC]) + bu[:, FFC * j : FFC * j + FFC]
        half = 0.5 * (1.0 + lax.erf(u * (1.0 / math.sqrt(2.0))))
        act = (u * half).astype(bf16)
        FAB[512 * j : 512 * j + 512, :] = act
        slope = half + u * (jnp.exp(u * u * -0.5) * (1.0 / math.sqrt(2.0 * math.pi)))
        FAB[3072 + 512 * j : 3072 + 512 * j + 512, :] = slope.astype(bf16)
        ffn_loads[n][1].wait()
        y = dot_nn(act, WS[a + 1, :FFC, :])
        T2[...] = y if n == 0 else T2[...] + y
        ffn_loads[n + 2] = load_ffn(n + 2, ffn_order[n + 2])

    ld_c.wait()
    sums = [jnp.zeros((8, D), f32)] * 3
    for r in range(0, rows, BR):
        rs = slice(r, r + BR)
        r2 = (T1[rs, :] * g1[...] + b1[...]) + (T2[rs, :] + bd[...])
        cen = r2 - jnp.mean(r2, axis=1, keepdims=True)
        rstd = lax.rsqrt(jnp.mean(cen * cen, axis=1, keepdims=True) + EPSILON)
        xh = cen * rstd
        DO[rs, :] = (xh * g2[...] + b2[...]).astype(bf16)
        dy = CD[rs, :].astype(f32)
        dx = dy * g2[...]
        g = rstd * (dx - jnp.mean(dx, axis=1, keepdims=True) - xh * jnp.mean(dx * xh, axis=1, keepdims=True))
        T2[rs, :] = g
        gl = g.astype(bf16)
        G[rs, :] = gl
        sums = [sums[0] + fold8(dy * xh), sums[1] + fold8(dy), sums[2] + fold8(gl.astype(f32))]
    enc_copy = load(DO, enc_o.at[0], osem.at[0])
    for row, s in zip((ROW_FGAIN, ROW_FSHIFT, ROW_D), sums):
        b_acc[0, row : row + 1, :] = jnp.sum(s, axis=0, keepdims=True)

    for t in range(3):
        for j in range(6):
            w = dot_tn(FAB[512 * j : 512 * j + 512, :], G[:, 256 * t : 256 * t + 256]).astype(bf16)
            at = 512 * j
            while at < 512 * j + 512:
                seg, off = divmod(at, 96)
                size = min(96 - off, 512 * j + 512 - at)
                i, half = divmod(seg, 2)
                DU[pick(half, t, 6 + t), i // 8, (i // 4) % 2, (i // 2) % 2, i % 2, off : off + size, :] = w[
                    at - 512 * j : at - 512 * j + size
                ]
                at += size
        pieces["D%d" % t].start()

    e_in = {}

    def load_e(h):
        e_in[h] = load(e_hbm.at[h], FAB.at[pl.ds(1024 * (h % 3), 1024), :], esem.at[h % 3])

    for h in range(3):
        load_e(h)

    for n in range(6, 12):
        j = ffn_order[n]
        a = 2 * (n % 2)
        hf, t = divmod(j, 3)
        frow = slice(3072 + 512 * j, 3072 + 512 * j + 512)
        ffn_loads[n][1].wait()
        gi32 = dot_nt(G[...], WS[a + 1, :FFC, :]) * FAB[frow, :].astype(f32)
        gi = gi32.astype(bf16)
        FAB[frow, :] = gi
        s = jnp.sum(fold8(gi.astype(f32)), axis=0, keepdims=True)
        at = 512 * j
        while at < 512 * j + 512:
            row, off = divmod(at, D)
            size = min(D - off, 512 * j + 512 - at)
            b_acc[0, ROW_U + row : ROW_U + row + 1, off : off + size] = s[:, at - 512 * j : at - 512 * j + size]
            at += size
        w = dot_tn(HL[...], gi).astype(bf16)
        if hf == 0:
            pieces["D%d" % t].sent(0)
        dst = pick(hf, 3 + t, 6 + t)
        for i in range(16):
            where = (dst, i // 8, (i // 4) % 2, (i // 2) % 2, i % 2)
            DU[where + (slice(0, 48),)] = w[48 * i : 48 * i + 48, :256]
            DU[where + (slice(48, 96),)] = w[48 * i : 48 * i + 48, 256:]
        if hf == 1:
            pieces["U%d" % t].start()
        ffn_loads[n][0].wait()
        y = dot_nt(gi, WS[a, :, :FFC])
        T3[...] = (T2[...] if n == 6 else T3[...]) + y
        if n + 2 < 12:
            ffn_loads[n + 2] = load_ffn(n + 2, ffn_order[n + 2])
        step(*HOOK_FFN[n - 6])

    ld_q = load(wq_h, WS.at[0], wsem.at[0])
    ld_k = load(wk_h, WS.at[1], wsem.at[1])
    ld_v = load(wv_h, WS.at[2], wsem.at[2])

    sums = [jnp.zeros((8, D), f32)] * 3
    for r in range(0, rows, BR):
        rs = slice(r, r + BR)
        gh = T3[rs, :]
        xh = T1[rs, :]
        dx = gh * g1[...]
        g = RSTD[rs, :] * (dx - jnp.mean(dx, axis=1, keepdims=True) - xh * jnp.mean(dx * xh, axis=1, keepdims=True))
        T3[rs, :] = g
        gl = g.astype(bf16)
        G[rs, :] = gl
        sums = [sums[0] + fold8(gh * xh), sums[1] + fold8(gh), sums[2] + fold8(gl.astype(f32))]
    for row, s in zip((ROW_AGAIN, ROW_ASHIFT, ROW_O), sums):
        b_acc[0, row : row + 1, :] = jnp.sum(s, axis=0, keepdims=True)
    step(*HOOK_NORM)

    w = dot_tn(MIX[...], G[...]).astype(bf16)
    for half in range(2):
        for t in range(3):
            at = 384 * half + 128 * t
            OB[pick(half, 0, 1), t] = w[:, at : at + 128].reshape(2, 2, 2, 2, 48, 128)
    for t in range(3):
        pieces["O%d" % t].start()
    enc_copy.wait()
    DO[...] = dot_nt(G[...], WO[...]).astype(bf16)

    KT, KTP, VT, VTP = 3072, 3072 + D, 3072 + 2 * D, 3072 + 3 * D
    back = []
    for p in range(HEADS // 2):
        ls = slice(128 * p, 128 * p + 128)
        ps = 128 * p
        dos = DO[:, ls].astype(f32) * LINV[:, ls]
        extra = pltpu.roll(dos * MIX[:, ls].astype(f32), 64, 1) * -1.0
        dos = dos.astype(bf16)
        extra = extra.astype(bf16)
        dos_t = dos.T
        q_t = Q[:, ls].T
        dq = []
        for j in range(2):
            h = 2 * p + j
            base = 1024 * (h % 3)
            e_in.pop(h).wait()
            d_ext = own_lanes(j, dos, extra)
            rt = slice(64 * j, 64 * j + 64)
            acc = None
            for half, (k, v, kt, vt) in enumerate(((KO, VO, KT, VT), (KP, VP, KTP, VTP))):
                e = FAB[base + 512 * half : base + 512 * half + 512, :]
                dp = dot_nt(d_ext, own_lanes(j, v[:, ls], one))
                ds = (e.astype(f32) * dp).astype(bf16)
                x = dot_nn(ds, k[:, ls])
                acc = x if acc is None else acc + x
                FAB[vt + ps + 64 * j : vt + ps + 64 * j + 64, :] = dot_nn(dos_t[rt], e).astype(bf16)
                FAB[kt + ps + 64 * j : kt + ps + 64 * j + 64, :] = (dot_nn(q_t[rt], ds) * LN2).astype(bf16)
            dq.append(acc)
            if h + 3 < HEADS:
                load_e(h + 3)
            step(*HOOK_HEAD[h])
        CD[:, ls] = (jnp.where(low, dq[0], dq[1]) * scale).astype(bf16)
        for i, (src, dst) in enumerate(((KTP, KR), (VTP, VR))):
            cp = pltpu.make_async_remote_copy(
                FAB.at[pl.ds(src + ps, 128), :], dst.at[pl.ds(ps, 128), :], ksem_s.at[p, i], ksem_r.at[p, i],
                device_id=peer_of("c"), device_id_type=MESH,
            )
            cp.start()
            back.append(cp)

    def projection(t, grad):
        w = dot_tn(X[...], grad).astype(bf16)
        for half in range(2):
            QB[pick(half, 0, 1), t] = w[:, 384 * half : 384 * half + 384].reshape(2, 2, 2, 2, 48, 384)
        pieces["QKV"[t]].start()

    projection(0, CD[...])
    for cp in back:
        cp.wait_recv()
    HL[...] = (FAB[KT : KT + D, :].astype(f32) + KR[...].astype(f32)).astype(bf16).T
    projection(1, HL[...])
    G[...] = (FAB[VT : VT + D, :].astype(f32) + VR[...].astype(f32)).astype(bf16).T
    projection(2, G[...])
    b_acc[0, ROW_Q : ROW_Q + 1, :] = jnp.sum(fold8(CD[...].astype(f32)), axis=0, keepdims=True)
    b_acc[0, ROW_V : ROW_V + 1, :] = jnp.sum(fold8(G[...].astype(f32)), axis=0, keepdims=True)
    b_acc[0, 12:16, :] = jnp.zeros((4, D), f32)
    vec = []

    def vec_start(k):
        cp = pltpu.make_async_remote_copy(
            b_acc.at[k], b_recv.at[k], ssem.at[N_PIECES, k], rsem.at[N_PIECES, k],
            device_id=peer_of(BITS[k]), device_id_type=MESH,
        )
        cp.start()
        vec.append(cp)

    def vec_step(k):
        vec[k].wait_recv()
        b_acc[k + 1] = b_acc[k] + b_recv[k]
        if k < 4:
            vec_start(k + 1)

    vec_start(0)
    step(*HOOK_PROJ)
    vec_step(0)
    ld_q.wait()
    ld_k.wait()
    ld_v.wait()
    total = T3[...] + dot_nt(CD[...], WS[0]) + dot_nt(HL[...], WS[1]) + dot_nt(G[...], WS[2])
    MIX[...] = total.astype(bf16)
    tg_copy = load(MIX, tg_o.at[0], osem.at[1])

    for group in HOOK_TAIL:
        for name, k in group:
            if name == "vec":
                vec_step(k)
            else:
                pieces[name].finish(k)
    vec_copy = load(b_acc.at[5], vec_o, osem.at[2])

    outs = []
    for i, name in enumerate(NAMES):
        pc = pieces[name]
        for side, half in ((0, c), (1, 1 - c)):
            src = pc.fin[side]
            if side:
                pc.cp[5].wait_recv()
            sem = osem.at[3 + 2 * i + side]
            if name[0] == "D":
                t = int(name[1])
                outs.append(load(src, dg_o.at[pl.ds(pl.multiple_of(half * 96, 96), 96), pl.ds(256 * t, 256)], sem))
            elif name[0] == "U":
                col = half * 1536 + int(name[1]) * 512
                outs.append(load(src.at[pl.ds(0, 48)], ug_o.at[:, pl.ds(pl.multiple_of(col, 256), 256)], sem))
                sem2 = osem.at[3 + 2 * N_PIECES + 2 * i + side]
                outs.append(load(src.at[pl.ds(48, 48)], ug_o.at[:, pl.ds(pl.multiple_of(col + 256, 256), 256)], sem2))
            elif name[0] == "O":
                outs.append(load(src, og_o.at[:, pl.ds(pl.multiple_of(half * 384 + int(name[1]) * 128, 128), 128)], sem))
            else:
                dst = (qg_o, kg_o, vg_o)["QKV".index(name)]
                outs.append(load(src, dst.at[:, pl.ds(pl.multiple_of(half * 384, 128), 384)], sem))
    for cp in outs:
        cp.wait()
    vec_copy.wait()
    tg_copy.wait()
    send_k.wait_send()
    send_v.wait_send()
    for cp in back:
        cp.wait_send()
    for cp in vec:
        cp.wait_send()
    for name in NAMES:
        for k in range(6):
            if k not in pieces[name].done:
                pieces[name].sent(k)


HOOK_FFN = [[], [("D0", 0)], [("D1", 0)], [("D2", 0)], [("U0", 0)], []]
HOOK_NORM = [("U1", 0)]
HOOK_HEAD = {h: [] for h in range(HEADS)}
HOOK_HEAD[0] = [("U2", 0)]
HOOK_HEAD[1] = [("O0", 0), ("O1", 0), ("O2", 0)]
HOOK_HEAD[2] = [("D0", 1), ("D1", 1), ("D2", 1)]
HOOK_HEAD[4] = [("U0", 1), ("U1", 1), ("U2", 1)]
HOOK_HEAD[6] = [("D0", 2), ("D1", 2), ("D2", 2)]
HOOK_HEAD[7] = [("O0", 1), ("O1", 1), ("O2", 1)]
HOOK_HEAD[8] = [("D0", 3), ("D1", 3), ("D2", 3)]
HOOK_HEAD[10] = [("U0", 2), ("U1", 2), ("U2", 2)]
HOOK_HEAD[11] = [("O0", 2), ("O1", 2), ("O2", 2), ("D0", 4), ("D1", 4), ("D2", 4)]
HOOK_PROJ = [("Q", 0), ("K", 0), ("V", 0)]
HOOK_TAIL = [
    [("U0", 3), ("U1", 3), ("U2", 3), ("vec", 1), ("O0", 3), ("O1", 3), ("O2", 3), ("vec", 2)],
    [("U0", 4), ("U1", 4), ("U2", 4), ("vec", 3), ("O0", 4), ("O1", 4), ("O2", 4), ("vec", 4)],
    [("Q", 1), ("K", 1), ("V", 1)],
    [("Q", 2), ("K", 2), ("V", 2)],
    [("Q", 3), ("K", 3), ("V", 3)],
    [("Q", 4), ("K", 4), ("V", 4)],
]


def layer_call(tokens, lengths, cotangent, wq, bq, wk, wv, bv, wo, bo, g1, b1, wu, bu, wd, bd, g2, b2):
    rows, D = tokens.shape[1:]
    row = lambda v: v.reshape(1, -1)
    lead = (2, 2, 2, 2)

    def ladder(n, R, C):
        return tuple(pltpu.VMEM((n,) + (2,) * (4 - k) + (R, C), bf16) for k in range(1, 5))

    big = pltpu.VMEM((rows, D), f32)
    low = pltpu.VMEM((rows, D), bf16)
    wide = pltpu.VMEM((D, D), bf16)
    scratch = [
        low, pltpu.VMEM((4, D, D), bf16), wide, low, low, low, low, low, pltpu.VMEM((2, rows, 128), bf16), low, big,
        big, big, big, pltpu.VMEM((rows, 1), f32), low, low, low, low, pltpu.VMEM((6144, 512), bf16),
        pltpu.VMEM((D, rows), bf16), pltpu.VMEM((D, rows), bf16),
        pltpu.VMEM((9,) + lead + (96, 256), bf16), pltpu.VMEM((2, 3) + lead + (48, 128), bf16),
        pltpu.VMEM((2, 3) + lead + (48, 384), bf16),
        pltpu.VMEM((6,) + lead + (96, 256), bf16), pltpu.VMEM((3,) + lead + (48, 128), bf16),
        pltpu.VMEM((3,) + lead + (48, 384), bf16),
        ladder(6, 96, 256), ladder(3, 48, 128), ladder(3, 48, 384),
        pltpu.VMEM((6, 2, 96, 256), f32), pltpu.VMEM((3, 2, 48, 128), f32), pltpu.VMEM((3, 2, 48, 384), f32),
        pltpu.VMEM((6, 16, D), f32), pltpu.VMEM((5, 16, D), f32),
        pltpu.SemaphoreType.DMA((7,)), pltpu.SemaphoreType.DMA((6,)), pltpu.SemaphoreType.DMA((3 + 4 * N_PIECES,)),
        pltpu.SemaphoreType.DMA((7, 2)), pltpu.SemaphoreType.DMA((7, 2)),
        pltpu.SemaphoreType.DMA((N_PIECES + 1, 6)), pltpu.SemaphoreType.DMA((N_PIECES + 1, 6)),
    ]
    hbm = pl.BlockSpec(memory_space=pl.ANY)
    vm = pl.BlockSpec(memory_space=pltpu.VMEM)
    sm = pl.BlockSpec(memory_space=pltpu.SMEM)
    specs = [hbm, sm, hbm, hbm, vm, hbm, hbm, vm, hbm, vm, vm, vm, hbm, vm, hbm, vm, vm, vm]
    sds = jax.ShapeDtypeStruct
    shapes = [sds(tokens.shape, bf16), sds(tokens.shape, bf16)] + [sds((48, D), f32)] * 4 + [
        sds((48, 4 * D), f32), sds((192, D), f32), sds((16, D), f32), sds((HEADS, 1024, 512), bf16)]
    return pl.pallas_call(
        layer_kernel,
        out_shape=shapes,
        in_specs=specs,
        out_specs=[hbm] * len(shapes),
        scratch_shapes=scratch,
        compiler_params=pltpu.CompilerParams(collective_id=0, has_side_effects=True, vmem_limit_bytes=VMEM_LIMIT),
    )(tokens, lengths, cotangent, wq, row(bq), wk, wv, row(bv), wo, row(bo), row(g1), row(b1), wu, row(bu), wd, row(bd),
      row(g2), row(b2))


VMEM_LIMIT = 64 << 20


def hand_on_kernel(*refs):
    n = 8
    vec = refs[n]
    outs = refs[n + 1 : 2 * n + 1]
    vecs = refs[2 * n + 1 : -1]
    sem = refs[-1]
    copies = []
    for i in range(n):
        cp = pltpu.make_async_copy(refs[i], outs[i], sem.at[i])
        cp.start()
        copies.append(cp)
    for ref, (row, count) in zip(vecs, VEC_ROWS):
        for k in range(count):
            ref[768 * k : 768 * k + 768] = vec[row + k]
    for cp in copies:
        cp.wait()


VEC_ROWS = ((ROW_Q, 1), (ROW_V, 1), (ROW_O, 1), (ROW_AGAIN, 1), (ROW_ASHIFT, 1), (ROW_U, 4), (ROW_D, 1), (ROW_FGAIN, 1),
            (ROW_FSHIFT, 1))


def hand_on(arrays, vec):
    hbm = pl.BlockSpec(memory_space=pl.ANY)
    vm = pl.BlockSpec(memory_space=pltpu.VMEM)
    return pl.pallas_call(
        hand_on_kernel,
        out_shape=[jax.ShapeDtypeStruct(a.shape, a.dtype) for a in arrays]
        + [jax.ShapeDtypeStruct((768 * n,), f32) for _, n in VEC_ROWS],
        in_specs=[hbm] * len(arrays) + [vm],
        out_specs=[hbm] * len(arrays) + [vm] * len(VEC_ROWS),
        scratch_shapes=[pltpu.SemaphoreType.DMA((len(arrays),))],
    )(*arrays, vec)


def on_device_fused(*args):
    enc, tg, qg, kg, vg, og, ug, dg, vec, _ = layer_call(*args)
    (enc, tg, qg, kg, vg, og, ug, dg, qb, vb, ob, ag, ash, ub, db, fg, fs) = hand_on(
        [enc, tg, qg, kg, vg, og, ug, dg], vec)
    return (enc, tg, qg, qb, kg, vg, vb, og, ob, ag, ash, ug, ub, dg, db, fg, fs)


CONTRACT_ROWS = (((0,), (0,)), ((), ()))
CONTRACT_COLS = (((1,), (1,)), ((), ()))


def norm_rows(values_in, gain_vec, shift_vec):
    row_mean = jnp.mean(values_in, axis=-1, keepdims=True)
    centred = values_in - row_mean
    spread = jnp.mean(centred * centred, axis=-1, keepdims=True)
    return centred * lax.rsqrt(spread + EPSILON) * gain_vec + shift_vec


def gelu_exact(values_in):
    return 0.5 * values_in * (1.0 + lax.erf(values_in * (1.0 / math.sqrt(2.0))))


def row_dot(left, right):
    return lax.dot_general(left, right, CONTRACT_ROWS, preferred_element_type=jnp.float32)


def col_dot(left, right):
    return lax.dot_general(left, right, CONTRACT_COLS, preferred_element_type=jnp.float32)


def heads_first(values_in):
    seq_count, positions, features = values_in.shape
    return jnp.moveaxis(values_in.reshape(seq_count, positions, HEADS, features // HEADS), 2, 0)


def heads_last(values_in):
    head_count, seq_count, positions, head_size = values_in.shape
    return jnp.moveaxis(values_in, 0, 2).reshape(seq_count, positions, head_count * head_size)


def column_sum(values_in):
    return jnp.sum(values_in.astype(jnp.float32), axis=0)


def on_device(
    tokens,
    lengths,
    cotangent,
    query_weight,
    query_bias,
    key_matrix,
    value_weight,
    value_bias,
    output_weight,
    output_bias,
    attn_gain,
    attn_shift,
    up_weight,
    up_bias,
    down_weight,
    down_bias,
    ffn_gain,
    ffn_shift,
):
    seq_count, seq_rows, features = tokens.shape
    key_total = seq_rows * lax.axis_size("blk")
    score_scale = 1.0 / math.sqrt(features // HEADS)
    flat_tokens = tokens.reshape(seq_count * seq_rows, features)
    counted = jnp.arange(key_total, dtype=jnp.int32)[None, None, :] < lengths[:, None, None]
    queries = (
        jnp.dot(flat_tokens, query_weight, preferred_element_type=jnp.float32) + query_bias
    ).astype(jnp.bfloat16)
    keyset = jnp.dot(flat_tokens, key_matrix, preferred_element_type=jnp.float32).astype(
        jnp.bfloat16
    )
    valset = (
        jnp.dot(flat_tokens, value_weight, preferred_element_type=jnp.float32) + value_bias
    ).astype(jnp.bfloat16)
    own_keys = keyset.reshape(seq_count, seq_rows, features)
    own_values = valset.reshape(seq_count, seq_rows, features)
    keys_all, values_all = (
        lax.all_gather(own_keys, "blk", axis=1, tiled=True),
        lax.all_gather(own_values, "blk", axis=1, tiled=True),
    )
    query_seq = queries.reshape(seq_count, seq_rows, features)
    query_heads = heads_first(query_seq)
    key_heads = heads_first(keys_all)
    value_heads = heads_first(values_all)

    def forward_head(pieces):
        single_query_head, single_key_head, single_value_head = pieces
        scores = (
            jnp.einsum(
                "pne,pme->pnm",
                single_query_head,
                single_key_head,
                preferred_element_type=jnp.float32,
            )
            * score_scale
        )
        masked = jnp.where(counted, scores, -1e30)
        largest = jnp.max(masked, axis=-1, keepdims=True)
        raised = jnp.exp(masked - largest)
        row_total = jnp.sum(raised, axis=-1, keepdims=True)
        reduced_probabilities = (raised / row_total).astype(jnp.bfloat16)
        mixed_head = jnp.einsum(
            "ocp,opn->ocn",
            reduced_probabilities,
            single_value_head,
            preferred_element_type=jnp.float32,
        )
        return (mixed_head.astype(jnp.bfloat16), (largest + jnp.log(row_total))[..., 0])

    mixed_heads, lse_heads = lax.map(forward_head, (query_heads, key_heads, value_heads))
    mixed_out = heads_last(mixed_heads).reshape(seq_count * seq_rows, features)
    attended = jnp.dot(mixed_out, output_weight, preferred_element_type=jnp.float32) + output_bias
    first_sum = flat_tokens.astype(jnp.float32) + attended
    hidden, attn_pull = jax.vjp(norm_rows, first_sum, attn_gain, attn_shift)
    hidden_low = hidden.astype(jnp.bfloat16)
    inner_act = jnp.dot(hidden_low, up_weight, preferred_element_type=jnp.float32) + up_bias
    gelu_value, gelu_pull = jax.vjp(gelu_exact, inner_act)
    active = gelu_value.astype(jnp.bfloat16)
    ffn_out = jnp.dot(active, down_weight, preferred_element_type=jnp.float32) + down_bias
    normalized_rows, ffn_pull = jax.vjp(norm_rows, hidden + ffn_out, ffn_gain, ffn_shift)
    encoded = normalized_rows.astype(jnp.bfloat16).reshape(seq_count, seq_rows, features)
    g_second, fgain_part, fshift_part = ffn_pull(
        cotangent.reshape(seq_count * seq_rows, features).astype(jnp.float32)
    )
    g_ffn = g_second.astype(jnp.bfloat16)
    dweight_part = row_dot(active, g_ffn)
    dbias_part = column_sum(g_ffn)
    (g_inner_wide,) = gelu_pull(col_dot(g_ffn, down_weight))
    g_inner = g_inner_wide.astype(jnp.bfloat16)
    uweight_part = row_dot(hidden_low, g_inner)
    ubias_part = column_sum(g_inner)
    g_hidden = g_second + col_dot(g_inner, up_weight)
    g_first, again_part, ashift_part = attn_pull(g_hidden)
    g_att = g_first.astype(jnp.bfloat16)
    oweight_part = row_dot(mixed_out, g_att)
    obias_part = column_sum(g_att)
    g_mixed = col_dot(g_att, output_weight).astype(jnp.bfloat16)
    keys_back, values_back = (
        lax.all_gather(own_keys, "blk", axis=1, tiled=True),
        lax.all_gather(own_values, "blk", axis=1, tiled=True),
    )
    key_back_heads = heads_first(keys_back)
    value_back_heads = heads_first(values_back)
    g_mixed_seq = g_mixed.reshape(seq_count, seq_rows, features)
    grad_mixed_heads = heads_first(g_mixed_seq)

    def backward_head(pieces):
        single_query_head, single_key_head, single_value_head, lse_head, head_gradient = pieces
        scores = (
            jnp.einsum(
                "pne,pme->pnm",
                single_query_head,
                single_key_head,
                preferred_element_type=jnp.float32,
            )
            * score_scale
        )
        soft_probs = jnp.where(counted, jnp.exp(scores - lse_head[..., None]), 0.0)
        reduced_probabilities = soft_probs.astype(jnp.bfloat16)
        grad_value = jnp.einsum(
            "xwr,xwa->xra", reduced_probabilities, head_gradient, preferred_element_type=jnp.float32
        )
        grad_probs = jnp.einsum(
            "pne,pme->pnm", head_gradient, single_value_head, preferred_element_type=jnp.float32
        )
        row_inner = jnp.sum(soft_probs * grad_probs, axis=-1, keepdims=True)
        score_gradient = (soft_probs * (grad_probs - row_inner)).astype(jnp.bfloat16)
        grad_query = (
            jnp.einsum(
                "ocp,opn->ocn", score_gradient, single_key_head, preferred_element_type=jnp.float32
            )
            * score_scale
        )
        grad_key = (
            jnp.einsum(
                "xwr,xwa->xra",
                score_gradient,
                single_query_head,
                preferred_element_type=jnp.float32,
            )
            * score_scale
        )
        return (grad_query, grad_key, grad_value)

    query_grads, key_grads, value_grads = lax.map(
        backward_head, (query_heads, key_back_heads, value_back_heads, lse_heads, grad_mixed_heads)
    )
    key_grads_own, value_grads_own = (
        lax.psum_scatter(
            heads_last(key_grads).astype(jnp.bfloat16), "blk", scatter_dimension=1, tiled=True
        ).astype(jnp.float32),
        lax.psum_scatter(
            heads_last(value_grads).astype(jnp.bfloat16), "blk", scatter_dimension=1, tiled=True
        ).astype(jnp.float32),
    )
    g_query = heads_last(query_grads).reshape(seq_count * seq_rows, features).astype(jnp.bfloat16)
    g_key = key_grads_own.reshape(seq_count * seq_rows, features).astype(jnp.bfloat16)
    g_value = value_grads_own.reshape(seq_count * seq_rows, features).astype(jnp.bfloat16)
    qweight_part = row_dot(flat_tokens, g_query)
    qbias_part = column_sum(g_query)
    kweight_part = row_dot(flat_tokens, g_key)
    vweight_part = row_dot(flat_tokens, g_value)
    vbias_part = column_sum(g_value)
    token_wide = (
        g_first
        + col_dot(g_query, query_weight)
        + col_dot(g_key, key_matrix)
        + col_dot(g_value, value_weight)
    )
    token_grad = token_wide.astype(jnp.bfloat16).reshape(seq_count, seq_rows, features)
    qrow, krow, vrow, orow, urow, drow = (
        lax.psum_scatter(
            qweight_part.astype(jnp.bfloat16), "dp", scatter_dimension=0, tiled=True
        ).astype(jnp.float32),
        lax.psum_scatter(
            kweight_part.astype(jnp.bfloat16), "dp", scatter_dimension=0, tiled=True
        ).astype(jnp.float32),
        lax.psum_scatter(
            vweight_part.astype(jnp.bfloat16), "dp", scatter_dimension=0, tiled=True
        ).astype(jnp.float32),
        lax.psum_scatter(
            oweight_part.astype(jnp.bfloat16), "dp", scatter_dimension=0, tiled=True
        ).astype(jnp.float32),
        lax.psum_scatter(
            uweight_part.astype(jnp.bfloat16), "dp", scatter_dimension=0, tiled=True
        ).astype(jnp.float32),
        lax.psum_scatter(
            dweight_part.astype(jnp.bfloat16), "dp", scatter_dimension=0, tiled=True
        ).astype(jnp.float32),
    )
    qfinal, kfinal, vfinal, ofinal, ufinal, dfinal = (
        lax.psum(qrow.astype(jnp.bfloat16), "blk").astype(jnp.float32),
        lax.psum(krow.astype(jnp.bfloat16), "blk").astype(jnp.float32),
        lax.psum(vrow.astype(jnp.bfloat16), "blk").astype(jnp.float32),
        lax.psum(orow.astype(jnp.bfloat16), "blk").astype(jnp.float32),
        lax.psum(urow.astype(jnp.bfloat16), "blk").astype(jnp.float32),
        lax.psum(drow.astype(jnp.bfloat16), "blk").astype(jnp.float32),
    )
    (
        qbias_sum,
        vbias_sum,
        obias_sum,
        again_sum,
        ashift_sum,
        ubias_sum,
        dbias_sum,
        fgain_sum,
        fshift_sum,
    ) = lax.psum(
        (
            qbias_part,
            vbias_part,
            obias_part,
            again_part,
            ashift_part,
            ubias_part,
            dbias_part,
            fgain_part,
            fshift_part,
        ),
        ("dp", "blk"),
    )
    return (
        encoded,
        token_grad,
        qfinal,
        qbias_sum,
        kfinal,
        vfinal,
        vbias_sum,
        ofinal,
        obias_sum,
        again_sum,
        ashift_sum,
        ufinal,
        ubias_sum,
        dfinal,
        dbias_sum,
        fgain_sum,
        fshift_sum,
    )


def solution(mesh):
    return jax.shard_map(
        on_device_fused if dict(mesh.shape) == {"dp": 16, "blk": 2} else on_device,
        mesh=mesh,
        in_specs=(
            P("dp", "blk", None),
            P("dp"),
            P("dp", "blk", None),
            P(),
            P(),
            P(),
            P(),
            P(),
            P(),
            P(),
            P(),
            P(),
            P(),
            P(),
            P(),
            P(),
            P(),
            P(),
        ),
        out_specs=(
            P("dp", "blk", None),
            P("dp", "blk", None),
            P("dp", None),
            P(),
            P("dp", None),
            P("dp", None),
            P(),
            P("dp", None),
            P(),
            P(),
            P(),
            P("dp", None),
            P(),
            P("dp", None),
            P(),
            P(),
            P(),
        ),
        check_vma=False,
    )
```

```python
import math

import jax
import jax.numpy as jnp
from jax import lax
from jax.experimental import pallas as pl
from jax.experimental.pallas import tpu as pltpu
from jax.sharding import PartitionSpec as P

MESH = pl.DeviceIdType.MESH
f32, bf16 = jnp.float32, jnp.bfloat16

HEADS = 12
EPSILON = 1e-05

LOG2E = math.log2(math.e)
LN2 = math.log(2.0)
AX = {"zh": (3, 1), "zl": (2, 2), "y": (1, 3), "x": (0, 4)}
BITS = ("c", "x", "y", "zl", "zh")
ORDERS = (("x", "y", "zl", "zh"), ("y", "x", "zl", "zh"), ("zl", "x", "y", "zh"), ("zl", "y", "x", "zh"))
PIECES = (
    tuple(("D%d" % t, 96, 128, t % 3) for t in range(6))
    + tuple(("U%d" % t, 96, 128, (0, 1, 3)[t % 3]) for t in range(6))
    + tuple(("O%d" % t, 48, 128, t) for t in range(3))
    + tuple((n + str(t), 48, 128, (0, 1, 3 - t % 2)[i]) for t in range(3) for i, n in enumerate("QKV"))
)
NAMES = [p[0] for p in PIECES]
N_PIECES = len(PIECES)
ROW_O, ROW_AGAIN, ROW_ASHIFT, ROW_U, ROW_D, ROW_FGAIN, ROW_FSHIFT = 2, 3, 4, 5, 9, 10, 11
ROW_Q, ROW_V = 16, 17


def bit(dp, ax):
    return lax.rem(lax.div(dp, 1 << AX[ax][0]), 2)


def peer_of(ax):
    dp, c = lax.axis_index("dp"), lax.axis_index("blk")
    if ax == "c":
        return (dp, 1 - c)
    return (dp + (1 - 2 * bit(dp, ax)) * (1 << AX[ax][0]), c)


def dot_nn(a, b):
    return jnp.dot(a, b, preferred_element_type=f32)


def dot_nt(a, b):
    return lax.dot_general(a, b, (((1,), (1,)), ((), ())), preferred_element_type=f32)


def dot_tn(a, b):
    return lax.dot_general(a, b, (((0,), (0,)), ((), ())), preferred_element_type=f32)


def fold8(v):
    return jnp.sum(v.reshape(v.shape[0] // 8, 8, v.shape[1]), axis=0)


class Piece:
    def __init__(self, idx, own, other, recvs, fin, ssem, rsem):
        self.name, self.R, self.C, order = PIECES[idx]
        self.idx, self.own, self.other, self.recvs, self.fin = idx, own, other, recvs, fin
        self.ssem, self.rsem = ssem, rsem
        self.order = ORDERS[order]
        self.dp = lax.axis_index("dp")
        self.gone = set()

    def view(self, k, mine):
        idx = [slice(None)] * 4
        for j in range(k):
            ax = self.order[j]
            own = bit(self.dp, ax)
            idx[AX[ax][1] - 1] = own if (j < k - 1 or mine) else 1 - own
        return tuple(idx)

    def copy(self, k):
        if k == 0:
            src, ax = self.other, "c"
        else:
            src, ax = self.own.at[self.view(k, False)], self.order[k - 1]
        return pltpu.make_async_remote_copy(
            src, self.recvs[k], self.ssem.at[self.idx], self.rsem.at[self.idx, k], device_id=peer_of(ax), device_id_type=MESH
        )

    def start(self):
        self.copy(0).start()

    def sent(self, k):
        if k not in self.gone:
            self.copy(k).wait_send()
            self.gone.add(k)

    def finish(self, k):
        self.copy(k).wait_recv()
        self.sent(k)
        v = self.view(k, True)
        total = self.own[v].astype(f32) + self.recvs[k][...].astype(f32)
        if k < 4:
            self.own[v] = total.astype(bf16)
            self.copy(k + 1).start()
        else:
            self.fin[...] = total


class Vector:
    def __init__(self, idx, acc, recv, ssem, rsem):
        self.idx, self.acc, self.recv, self.ssem, self.rsem = idx, acc, recv, ssem, rsem

    def copy(self, k):
        return pltpu.make_async_remote_copy(
            self.acc.at[k], self.recv.at[k], self.ssem.at[self.idx], self.rsem.at[self.idx, k],
            device_id=peer_of(BITS[k]), device_id_type=MESH,
        )

    def start(self, k):
        self.copy(k).start()

    def step(self, k):
        self.copy(k).wait()
        self.acc[k + 1] = self.acc[k] + self.recv[k]
        if k < 4:
            self.start(k + 1)


def layer_kernel(*refs):
    (tok_h, len_s, cot_h, wq_h, bq, wk_h, wv_h, bv, wo_h, bo, g1, b1, wu_h, bu, wd_h, bd, g2, b2) = refs[:18]
    enc_o, tg_o, du_o, small_o, vec_o, e_hbm = refs[18:24]
    (X, WS, WO, Q, KO, KP, VO, VP, MB, MIX, LINV, T1, T2, T3, RSTD, HL, G, DO, CD, FAB, KR, VR,
     DU, SB, RDU, RS, SDU, SS, FDU, FS, b_acc, b_recv, l_acc, l_recv,
     VEC, LEN, wsem, vsem, esem, osem, ksem_s, ksem_r, ssem, rsem, fsem_s, fsem_r) = refs[24:]
    c = lax.axis_index("blk")
    rows = X.shape[0]
    D = X.shape[1]
    scale = 1.0 / math.sqrt(D // HEADS)

    def load(src, dst, sem):
        cp = pltpu.make_async_copy(src, dst, sem)
        cp.start()
        return cp

    ld_x = load(tok_h.at[0], X, wsem.at[5])
    ld_k = load(wk_h, WS.at[0], wsem.at[0])
    vec_in = (bq, bv, bo, g1, b1, bd, g2, b2, bu)
    ld_vec = [load(v, dst, vsem.at[i]) for i, (v, dst) in enumerate(zip(vec_in, VEC))]
    ld_len = load(len_s, LEN, vsem.at[9])
    ld_v = load(wv_h, WS.at[1], wsem.at[1])
    ld_q = load(wq_h, WS.at[2], wsem.at[2])

    barrier = pltpu.get_barrier_semaphore()
    for ax in BITS:
        pl.semaphore_signal(barrier, inc=1, device_id=peer_of(ax), device_id_type=MESH)

    def pick(half, mine, theirs):
        return jnp.where(half == c, mine, theirs)

    pieces = {}
    for i, (name, _, _, _) in enumerate(PIECES):
        if i < 12:
            own, other, recvs, fin = DU.at[i], DU.at[12 + i % 6], [r.at[i] for r in (RDU,) + SDU], FDU.at[i, c]
        else:
            k = i - 12
            own, other, recvs, fin = SB.at[0, k], SB.at[1, k], [r.at[k] for r in (RS,) + SS], FS.at[k, c]
        pieces[name] = Piece(i, own, other, recvs, fin, ssem, rsem)

    def step(label):
        for name, k in HOOKS.get(label, ()):
            if name == "early":
                early.step(k)
            elif name == "late":
                late.step(k)
            else:
                pieces[name].finish(k)
                if k == 4:
                    group = min(NAMES.index(name) // 6, 2)
                    left[group] -= 1
                    if not left[group]:
                        last_copy(group).start()

    left = [6, 6, 12]

    def last_copy(g):
        ref = (FDU.at[pl.ds(0, 6), c], FDU.at[pl.ds(6, 6), c], FS.at[:, c])[g]
        return pltpu.make_async_remote_copy(
            ref, ref, fsem_s.at[g], fsem_r.at[g], device_id=peer_of("c"), device_id_type=MESH
        )

    early = Vector(N_PIECES, b_acc, b_recv, ssem, rsem)
    late = Vector(N_PIECES + 1, l_acc, l_recv, ssem, rsem)
    b_acc[0] = jnp.zeros(b_acc.shape[1:], f32)

    lane = lax.broadcasted_iota(jnp.int32, (rows, 128), 1)
    low = lane < 64
    ld_len.wait()
    length = LEN[0]
    pos = lax.broadcasted_iota(jnp.int32, (rows, 128), 0)
    MB[0] = jnp.where(pos + c * rows < length, 0.0, -1e30).astype(bf16)
    MB[1] = jnp.where(pos + (1 - c) * rows < length, 0.0, -1e30).astype(bf16)

    def kv_send(src, dst, i):
        cp = pltpu.make_async_remote_copy(
            src.at[:, pl.ds(384 * (i % 2), 384)], dst.at[:, pl.ds(384 * (i % 2), 384)], ksem_s.at[6 + i], ksem_r.at[6 + i],
            device_id=peer_of("c"), device_id_type=MESH,
        )
        cp.start()
        return cp

    ld_x.wait()
    ld_k.wait()
    KO[...] = dot_nn(X[...], WS[0]).astype(bf16)
    pl.semaphore_wait(barrier, 5)
    kv = [kv_send(KO, KP, 0)]
    ld_o = load(wo_h, WO, wsem.at[4])
    ld_c = load(cot_h.at[0], CD, wsem.at[6])
    for cp in ld_vec:
        cp.wait()
    bq, bv, bo, g1, b1, bd, g2, b2, bu = (v[...].reshape(1, -1) for v in VEC)
    ld_v.wait()
    VO[...] = (dot_nn(X[...], WS[1]) + bv).astype(bf16)
    kv += [kv_send(VO, VP, 2), kv_send(KO, KP, 1), kv_send(VO, VP, 3)]
    FFC = 512

    def load_ffn(n, j):
        a = 2 * (n % 2)
        return (
            load(wu_h.at[:, pl.ds(FFC * j, FFC)], WS.at[a, :, pl.ds(0, FFC)], wsem.at[a]),
            load(wd_h.at[pl.ds(FFC * j, FFC), :], WS.at[a + 1, pl.ds(0, FFC), :], wsem.at[a + 1]),
        )

    ffn_order = [0, 1, 2, 3, 4, 5, 0, 3, 1, 4, 2, 5]
    ffn_loads = {0: load_ffn(0, ffn_order[0])}
    ld_q.wait()
    Q[...] = ((dot_nn(X[...], WS[2]) + bq) * (scale * LOG2E)).astype(bf16)

    one, zero = jnp.ones((rows, 128), bf16), jnp.zeros((rows, 128), bf16)
    hot = [jnp.where(lane == 64, 1.0, 0.0).astype(bf16), jnp.where(lane == 0, 1.0, 0.0).astype(bf16)]

    def own_lanes(j, mine, rest):
        return jnp.where(low, mine, rest) if j == 0 else jnp.where(low, rest, mine)

    def e_slot(row, h, n, sem, out):
        buf, far = FAB.at[pl.ds(row, 1024 * n), :], e_hbm.at[pl.ds(1024 * h, 1024 * n), :]
        return pltpu.make_async_copy(buf, far, sem) if out else pltpu.make_async_copy(far, buf, sem)

    def e_out(g):
        return e_slot(3072 * (g % 2), 3 * g, 3, esem.at[g % 2], True)

    res = []
    for h in range(HEADS):
        p, j = divmod(h, 2)
        g = h // 3
        ls = slice(128 * p, 128 * p + 128)
        if h == 0:
            kv[0].wait_recv()
            kv[1].wait_recv()
        if h == 6:
            kv[2].wait_recv()
            kv[3].wait_recv()
        if h % 3 == 0 and g >= 2:
            e_out(g - 2).wait()
        q = own_lanes(j, Q[:, ls], hot[j])
        s_o = dot_nt(q, own_lanes(j, KO[:, ls], MB[0]))
        s_p = dot_nt(q, own_lanes(j, KP[:, ls], MB[1]))
        m = jnp.maximum(jnp.max(s_o, axis=1, keepdims=True), jnp.max(s_p, axis=1, keepdims=True))
        e_o = jnp.exp2(s_o - m).astype(bf16)
        e_p = jnp.exp2(s_p - m).astype(bf16)
        base = 1024 * (h % 6)
        FAB[base : base + 512, :] = e_o
        FAB[base + 512 : base + 1024, :] = e_p
        res.append(dot_nn(e_o, own_lanes(j, VO[:, ls], one)) + dot_nn(e_p, own_lanes(j, VP[:, ls], one)))
        if j == 1:
            inv = 1.0 / pltpu.roll(jnp.where(low, res[1], res[0]), 64, 1)
            MIX[:, ls] = (jnp.where(low, res[0], res[1]) * inv).astype(bf16)
            LINV[:, ls] = inv
            res = []
        if h % 3 == 2:
            e_out(g).start()

    ld_o.wait()
    T2[...] = dot_nn(MIX[...], WO[...])
    BR = 128
    for r in range(0, rows, BR):
        rs = slice(r, r + BR)
        r1 = X[rs, :].astype(f32) + (T2[rs, :] + bo)
        cen = r1 - jnp.mean(r1, axis=1, keepdims=True)
        rstd = lax.rsqrt(jnp.mean(cen * cen, axis=1, keepdims=True) + EPSILON)
        xh = cen * rstd
        T1[rs, :] = xh
        RSTD[rs, :] = rstd
        HL[rs, :] = (xh * g1 + b1).astype(bf16)
    e_out(2).wait()
    e_out(3).wait()

    for n in range(6):
        j = ffn_order[n]
        a = 2 * (n % 2)
        ffn_loads[n][0].wait()
        ffn_loads[n][1].wait()
        ffn_loads[n + 1] = load_ffn(n + 1, ffn_order[n + 1])
        u = dot_nn(HL[...], WS[a, :, :FFC]) + bu[:, FFC * j : FFC * j + FFC]
        half = 0.5 * (1.0 + lax.erf(u * (1.0 / math.sqrt(2.0))))
        act = (u * half).astype(bf16)
        FAB[512 * j : 512 * j + 512, :] = act
        slope = half + u * (jnp.exp(u * u * -0.5) * (1.0 / math.sqrt(2.0 * math.pi)))
        FAB[3072 + 512 * j : 3072 + 512 * j + 512, :] = slope.astype(bf16)
        y = dot_nn(act, WS[a + 1, :FFC, :])
        T2[...] = y if n == 0 else T2[...] + y

    ld_c.wait()
    sums = [jnp.zeros((8, D), f32)] * 3
    for r in range(0, rows, BR):
        rs = slice(r, r + BR)
        r2 = (T1[rs, :] * g1 + b1) + (T2[rs, :] + bd)
        cen = r2 - jnp.mean(r2, axis=1, keepdims=True)
        rstd = lax.rsqrt(jnp.mean(cen * cen, axis=1, keepdims=True) + EPSILON)
        xh = cen * rstd
        DO[rs, :] = (xh * g2 + b2).astype(bf16)
        dy = CD[rs, :].astype(f32)
        dx = dy * g2
        g = rstd * (dx - jnp.mean(dx, axis=1, keepdims=True) - xh * jnp.mean(dx * xh, axis=1, keepdims=True))
        T2[rs, :] = g
        gl = g.astype(bf16)
        G[rs, :] = gl
        sums = [sums[0] + fold8(dy * xh), sums[1] + fold8(dy), sums[2] + fold8(gl.astype(f32))]
    enc_copy = load(DO, enc_o.at[0], osem.at[0])
    for row, s in zip((ROW_FGAIN, ROW_FSHIFT, ROW_D), sums):
        b_acc[0, row : row + 1, :] = jnp.sum(s, axis=0, keepdims=True)

    for t in range(3):
        for j in range(6):
            w = dot_tn(FAB[512 * j : 512 * j + 512, :], G[:, 256 * t : 256 * t + 256]).astype(bf16)
            at = 512 * j
            while at < 512 * j + 512:
                seg, off = divmod(at, 96)
                size = min(96 - off, 512 * j + 512 - at)
                i, half = divmod(seg, 2)
                for u in range(2):
                    where = (pick(half, 2 * t + u, 12 + 2 * t + u), i // 8, (i // 4) % 2, (i // 2) % 2, i % 2)
                    DU[where + (slice(off, off + size),)] = w[at - 512 * j : at - 512 * j + size, 128 * u : 128 * u + 128]
                at += size
        pieces["D%d" % (2 * t)].start()
        pieces["D%d" % (2 * t + 1)].start()
        step("D%d" % t)

    def e_in(h):
        slot = h % 4
        return e_slot((0, 1024, 2048, 6144)[slot], h, 1, esem.at[slot], False)

    for h in range(4):
        e_in(h).start()

    for n in range(6, 12):
        j = ffn_order[n]
        a = 2 * (n % 2)
        hf, t = divmod(j, 3)
        frow = slice(3072 + 512 * j, 3072 + 512 * j + 512)
        ffn_loads[n][0].wait()
        ffn_loads[n][1].wait()
        if n + 1 < 12:
            ffn_loads[n + 1] = load_ffn(n + 1, ffn_order[n + 1])
        gi32 = dot_nt(G[...], WS[a + 1, :FFC, :]) * FAB[frow, :].astype(f32)
        gi = gi32.astype(bf16)
        FAB[frow, :] = gi
        s = jnp.sum(fold8(gi.astype(f32)), axis=0, keepdims=True)
        at = 512 * j
        while at < 512 * j + 512:
            row, off = divmod(at, D)
            size = min(D - off, 512 * j + 512 - at)
            b_acc[0, ROW_U + row : ROW_U + row + 1, off : off + size] = s[:, at - 512 * j : at - 512 * j + size]
            at += size
        w = dot_tn(HL[...], gi).astype(bf16)
        if hf == 0:
            pieces["D%d" % (2 * t)].sent(0)
            pieces["D%d" % (2 * t + 1)].sent(0)
        for u in range(2):
            dst = pick(hf, 6 + 2 * t + u, 12 + 2 * t + u)
            for i in range(16):
                where = (dst, i // 8, (i // 4) % 2, (i // 2) % 2, i % 2)
                for v in range(2):
                    col = 256 * u + 128 * v
                    DU[where + (slice(48 * v, 48 * v + 48),)] = w[48 * i : 48 * i + 48, col : col + 128]
        y = dot_nt(gi, WS[a, :, :FFC])
        T3[...] = (T2[...] if n == 6 else T3[...]) + y
        if hf == 1:
            pieces["U%d" % (2 * t)].start()
            pieces["U%d" % (2 * t + 1)].start()
        step("F%d" % (n - 6))

    ld_q = load(wq_h, WS.at[0], wsem.at[0])
    ld_k = load(wk_h, WS.at[1], wsem.at[1])
    ld_v = load(wv_h, WS.at[2], wsem.at[2])

    sums = [jnp.zeros((8, D), f32)] * 3
    for r in range(0, rows, BR):
        rs = slice(r, r + BR)
        gh = T3[rs, :]
        xh = T1[rs, :]
        dx = gh * g1
        g = RSTD[rs, :] * (dx - jnp.mean(dx, axis=1, keepdims=True) - xh * jnp.mean(dx * xh, axis=1, keepdims=True))
        T3[rs, :] = g
        gl = g.astype(bf16)
        G[rs, :] = gl
        sums = [sums[0] + fold8(gh * xh), sums[1] + fold8(gh), sums[2] + fold8(gl.astype(f32))]
    for row, s in zip((ROW_AGAIN, ROW_ASHIFT, ROW_O), sums):
        b_acc[0, row : row + 1, :] = jnp.sum(s, axis=0, keepdims=True)
    early.start(0)
    step("N")

    w = dot_tn(MIX[...], G[...]).astype(bf16)
    for half in range(2):
        for t in range(3):
            at = 384 * half + 128 * t
            SB[pick(half, 0, 1), t] = w[:, at : at + 128].reshape(2, 2, 2, 2, 48, 128)
    for t in range(3):
        pieces["O%d" % t].start()
    step("M")
    enc_copy.wait()
    DO[...] = dot_nt(G[...], WO[...]).astype(bf16)

    step("P")

    def projection(m, t, grad):
        w = dot_tn(X[...], grad).astype(bf16)
        for half in range(2):
            SB[pick(half, 0, 1), 3 + 3 * t + m] = w[:, 128 * half : 128 * half + 128].reshape(2, 2, 2, 2, 48, 128)
        pieces["QKV"[m] + str(t)].start()

    def key_value(t):
        for i in range(2):
            back[2 * t + i].wait_recv()
        cs = slice(256 * t, 256 * t + 256)
        HL[:, cs] = (FAB[KT + 256 * t : KT + 256 * t + 256, :].astype(f32) + KR[cs, :].astype(f32)).astype(bf16).T
        projection(1, t, HL[:, cs])
        G[:, cs] = (FAB[VT + 256 * t : VT + 256 * t + 256, :].astype(f32) + VR[cs, :].astype(f32)).astype(bf16).T
        projection(2, t, G[:, cs])

    KT, KTP, VT, VTP = 3072, 3072 + D, 3072 + 2 * D, 3072 + 3 * D
    back = []
    for p in range(HEADS // 2):
        ls = slice(128 * p, 128 * p + 128)
        ps = 128 * p
        dos = DO[:, ls].astype(f32) * LINV[:, ls]
        extra = pltpu.roll(dos * MIX[:, ls].astype(f32), 64, 1) * -1.0
        dos = dos.astype(bf16)
        extra = extra.astype(bf16)
        dos_t = dos.T
        q_t = Q[:, ls].T
        dq = []
        e_in(2 * p).wait()
        e_in(2 * p + 1).wait()
        for j in range(2):
            h = 2 * p + j
            base = (0, 1024, 2048, 6144)[h % 4]
            d_ext = own_lanes(j, dos, extra)
            rt = slice(64 * j, 64 * j + 64)
            acc = None
            for half, (k, v, kt, vt) in enumerate(((KO, VO, KT, VT), (KP, VP, KTP, VTP))):
                e = FAB[base + 512 * half : base + 512 * half + 512, :]
                dp = dot_nt(d_ext, own_lanes(j, v[:, ls], one))
                ds = (e.astype(f32) * dp).astype(bf16)
                x = dot_nn(ds, k[:, ls])
                acc = x if acc is None else acc + x
                FAB[vt + ps + 64 * j : vt + ps + 64 * j + 64, :] = dot_nn(dos_t[rt], e).astype(bf16)
                FAB[kt + ps + 64 * j : kt + ps + 64 * j + 64, :] = (dot_nn(q_t[rt], ds) * LN2).astype(bf16)
            dq.append(acc)
        CD[:, ls] = (jnp.where(low, dq[0], dq[1]) * scale).astype(bf16)
        if p + 2 < HEADS // 2:
            e_in(2 * p + 4).start()
            e_in(2 * p + 5).start()
        t = p // 2
        if p % 2 == 1:
            for i, (src, dst) in enumerate(((KTP, KR), (VTP, VR))):
                cp = pltpu.make_async_remote_copy(
                    FAB.at[pl.ds(src + 256 * t, 256), :], dst.at[pl.ds(256 * t, 256), :],
                    ksem_s.at[2 * t + i], ksem_r.at[2 * t + i], device_id=peer_of("c"), device_id_type=MESH,
                )
                cp.start()
                back.append(cp)
            projection(0, t, CD[:, 256 * t : 256 * t + 256])
        elif t:
            key_value(t - 1)
        step("H%d" % p)

    key_value(2)
    late.acc[0, 0:1, :] = jnp.sum(fold8(CD[...].astype(f32)), axis=0, keepdims=True)
    late.acc[0, 1:2, :] = jnp.sum(fold8(G[...].astype(f32)), axis=0, keepdims=True)
    late.acc[0, 2:8, :] = jnp.zeros((6, D), f32)
    late.start(0)
    step("V")
    ld_q.wait()
    ld_k.wait()
    ld_v.wait()
    total = T3[...] + dot_nt(CD[...], WS[0]) + dot_nt(HL[...], WS[1]) + dot_nt(G[...], WS[2])
    MIX[...] = total.astype(bf16)
    tg_copy = load(MIX, tg_o.at[0], osem.at[1])

    step("T")
    vec_copies = [load(early.acc.at[5], vec_o.at[pl.ds(0, 16)], osem.at[2])]
    vec_copies.append(load(late.acc.at[5], vec_o.at[pl.ds(16, 8)], osem.at[3]))

    outs = []
    for g in range(3):
        last_copy(g).wait_recv()
    outs = [load(FDU, du_o, osem.at[4]), load(FS, small_o, osem.at[5])]
    for cp in outs:
        cp.wait()
    for cp in vec_copies:
        cp.wait()
    tg_copy.wait()
    for cp in kv + back:
        cp.wait_send()
    for g in range(3):
        last_copy(g).wait_send()


HOOKS = {
    "F0": (("D0", 0), ("D1", 0), ("D2", 0), ("D3", 0), ("D4", 0), ("D5", 0),),
    "F3": (("U0", 0), ("U1", 0),),
    "F5": (("U2", 0), ("U3", 0),),
    "N": (("D2", 1), ("D0", 1), ("D1", 1), ("D5", 1), ("U4", 0), ("U5", 0),),
    "M": (("early", 0), ("D3", 1), ("D4", 1),),
    "H0": (("O0", 0), ("O1", 0), ("O2", 0),),
    "H1": (("U2", 1), ("U1", 1),),
    "H2": (("D0", 2), ("Q0", 0), ("U5", 1), ("O2", 1),),
    "H3": (("early", 1), ("D3", 2), ("K0", 0), ("V0", 0),),
    "H4": (("D0", 3), ("O1", 1), ("Q1", 0), ("U0", 1),),
    "H5": (("D2", 2), ("D3", 3), ("U2", 2), ("U4", 1), ("K1", 0), ("D1", 2), ("V1", 0), ("D5", 2), ("V0", 1), ("early", 2), ("D0", 4),),
    "V": (("U5", 2), ("D4", 2), ("Q2", 0), ("O2", 2),),
    "T": (("K0", 1), ("K2", 0), ("late", 0), ("V2", 0), ("D3", 4), ("O0", 1), ("D1", 3), ("early", 3), ("D2", 3), ("U0", 2), ("U1", 2), ("O1", 2), ("O2", 3), ("D4", 3), ("D5", 3), ("U3", 1), ("V0", 2), ("V1", 1), ("Q0", 1), ("O0", 2), ("late", 1), ("U2", 3), ("K1", 1), ("D1", 4), ("U5", 3), ("O2", 4), ("K2", 1), ("D2", 4), ("K0", 2), ("V0", 3), ("late", 2), ("O1", 3), ("Q1", 1), ("D4", 4), ("Q0", 2), ("U3", 2), ("D5", 4), ("U4", 2), ("V1", 2), ("O0", 3), ("early", 4), ("U2", 4), ("Q2", 1), ("K1", 2), ("U0", 3), ("Q1", 2), ("K2", 2), ("V2", 1), ("U1", 3), ("V0", 4), ("O1", 4), ("U5", 4), ("K0", 3), ("V1", 3), ("late", 3), ("Q0", 3), ("O0", 4), ("Q2", 2), ("V2", 2), ("K1", 3), ("V2", 3), ("K0", 4), ("U0", 4), ("Q1", 3), ("V1", 4), ("K2", 3), ("U1", 4), ("U3", 3), ("Q0", 4), ("U4", 3), ("late", 4), ("Q2", 3), ("K1", 4), ("V2", 4), ("Q1", 4), ("K2", 4), ("Q2", 4), ("U3", 4), ("U4", 4),),
}


def layer_call(tokens, lengths, cotangent, wq, bq, wk, wv, bv, wo, bo, g1, b1, wu, bu, wd, bd, g2, b2):
    rows, D = tokens.shape[1:]
    lead = (2, 2, 2, 2)

    def ladder(n, R, C):
        return tuple(pltpu.VMEM((n,) + (2,) * (4 - k) + (R, C), bf16) for k in range(1, 5))

    big = pltpu.VMEM((rows, D), f32)
    low = pltpu.VMEM((rows, D), bf16)
    wide = pltpu.VMEM((D, D), bf16)
    scratch = [
        low, pltpu.VMEM((4, D, D), bf16), wide, low, low, low, low, low, pltpu.VMEM((2, rows, 128), bf16), low, big,
        big, big, big, pltpu.VMEM((rows, 1), f32), low, low, low, low, pltpu.VMEM((7168, 512), bf16),
        pltpu.VMEM((D, rows), bf16), pltpu.VMEM((D, rows), bf16),
        pltpu.VMEM((18,) + lead + (96, 128), bf16), pltpu.VMEM((2, 12) + lead + (48, 128), bf16),
        pltpu.VMEM((12,) + lead + (96, 128), bf16), pltpu.VMEM((12,) + lead + (48, 128), bf16),
        ladder(12, 96, 128), ladder(12, 48, 128),
        pltpu.VMEM((12, 2, 96, 128), f32), pltpu.VMEM((12, 2, 48, 128), f32),
        pltpu.VMEM((6, 16, D), f32), pltpu.VMEM((5, 16, D), f32), pltpu.VMEM((6, 8, D), f32), pltpu.VMEM((5, 8, D), f32),
        (pltpu.VMEM((D,), f32),) * 8 + (pltpu.VMEM((4 * D,), f32),), pltpu.SMEM((1,), jnp.int32),
        pltpu.SemaphoreType.DMA((7,)), pltpu.SemaphoreType.DMA((10,)), pltpu.SemaphoreType.DMA((4,)),
        pltpu.SemaphoreType.DMA((6,)), pltpu.SemaphoreType.DMA((10,)), pltpu.SemaphoreType.DMA((10,)),
        pltpu.SemaphoreType.DMA((N_PIECES + 2,)), pltpu.SemaphoreType.DMA((N_PIECES + 2, 5)),
        pltpu.SemaphoreType.DMA((3,)), pltpu.SemaphoreType.DMA((3,)),
    ]
    hbm = pl.BlockSpec(memory_space=pl.ANY)
    sds = jax.ShapeDtypeStruct
    shapes = [sds(tokens.shape, bf16), sds(tokens.shape, bf16), sds((12, 2, 96, 128), f32), sds((12, 2, 48, 128), f32),
              sds((24, D), f32), sds((HEADS * 1024, 512), bf16)]
    return pl.pallas_call(
        layer_kernel,
        out_shape=shapes,
        in_specs=[hbm] * 18,
        out_specs=[hbm] * len(shapes),
        scratch_shapes=scratch,
        compiler_params=pltpu.CompilerParams(collective_id=0, has_side_effects=True, vmem_limit_bytes=VMEM_LIMIT),
    )(tokens, lengths, cotangent, wq, bq, wk, wv, bv, wo, bo, g1, b1, wu, bu, wd, bd,
      g2, b2)


VMEM_LIMIT = 64 << 20


def hand_on_kernel(enc, tg, du, small, vec, *refs):
    outs, vecs = refs[:8], refs[8 : 8 + len(VEC_ROWS)]
    stage, done, sem = refs[8 + len(VEC_ROWS) : -7], refs[-7:-1], refs[-1]
    ins = [pltpu.make_async_copy(r, s, sem.at[i]) for i, (r, s) in enumerate(zip((enc, tg, du, small, vec), stage))]
    for cp in ins:
        cp.start()
    back = [pltpu.make_async_copy(s, o, sem.at[5 + i]) for i, (s, o) in enumerate(zip(stage[:2] + done, outs))]
    for i in range(2):
        ins[i].wait()
        back[i].start()
    q, k, v, o, u, d = done
    ins[2].wait()
    for t in range(6):
        for half in range(2):
            d[96 * half : 96 * half + 96, 128 * t : 128 * t + 128] = stage[2][t, half]
            for w in range(2):
                col = 1536 * half + 256 * t + 128 * w
                u[:, col : col + 128] = stage[2][6 + t, half, 48 * w : 48 * w + 48]
    back[7].start()
    back[6].start()
    ins[3].wait()
    for t in range(3):
        for half in range(2):
            o[:, 384 * half + 128 * t : 384 * half + 128 * t + 128] = stage[3][t, half]
            for m, w in enumerate((q, k, v)):
                w[:, 128 * half + 256 * t : 128 * half + 256 * t + 128] = stage[3][3 + 3 * t + m, half]
    for i in range(2, 6):
        back[i].start()
    ins[4].wait()
    for ref, (row, count) in zip(vecs, VEC_ROWS):
        for k in range(count):
            ref[768 * k : 768 * k + 768] = stage[4][row + k]
    for cp in back:
        cp.wait()


VEC_ROWS = ((ROW_Q, 1), (ROW_V, 1), (ROW_O, 1), (ROW_AGAIN, 1), (ROW_ASHIFT, 1), (ROW_U, 4), (ROW_D, 1), (ROW_FGAIN, 1),
            (ROW_FSHIFT, 1))


def hand_on(arrays):
    hbm = pl.BlockSpec(memory_space=pl.ANY)
    vm = pl.BlockSpec(memory_space=pltpu.VMEM)
    shapes = [(a.shape, a.dtype) for a in arrays[:2]] + [((48, 768), f32)] * 4 + [((48, 3072), f32), ((192, 768), f32)]
    return pl.pallas_call(
        hand_on_kernel,
        out_shape=[jax.ShapeDtypeStruct(*a) for a in shapes] + [jax.ShapeDtypeStruct((768 * k,), f32) for _, k in VEC_ROWS],
        in_specs=[hbm] * 5,
        out_specs=[hbm] * 8 + [vm] * len(VEC_ROWS),
        scratch_shapes=[pltpu.VMEM(a.shape, a.dtype) for a in arrays] + [pltpu.VMEM(*a) for a in shapes[2:]]
        + [pltpu.SemaphoreType.DMA((13,))],
        compiler_params=pltpu.CompilerParams(vmem_limit_bytes=VMEM_LIMIT),
    )(*arrays)


def on_device_fused(*args):
    (enc, tg, qg, kg, vg, og, ug, dg, qb, vb, ob, ag, ash, ub, db, fg, fs) = hand_on(layer_call(*args)[:5])
    return (enc, tg, qg, qb, kg, vg, vb, og, ob, ag, ash, ug, ub, dg, db, fg, fs)


CONTRACT_ROWS = (((0,), (0,)), ((), ()))
CONTRACT_COLS = (((1,), (1,)), ((), ()))


def norm_rows(values_in, gain_vec, shift_vec):
    row_mean = jnp.mean(values_in, axis=-1, keepdims=True)
    centred = values_in - row_mean
    spread = jnp.mean(centred * centred, axis=-1, keepdims=True)
    return centred * lax.rsqrt(spread + EPSILON) * gain_vec + shift_vec


def gelu_exact(values_in):
    return 0.5 * values_in * (1.0 + lax.erf(values_in * (1.0 / math.sqrt(2.0))))


def row_dot(left, right):
    return lax.dot_general(left, right, CONTRACT_ROWS, preferred_element_type=jnp.float32)


def col_dot(left, right):
    return lax.dot_general(left, right, CONTRACT_COLS, preferred_element_type=jnp.float32)


def heads_first(values_in):
    seq_count, positions, features = values_in.shape
    return jnp.moveaxis(values_in.reshape(seq_count, positions, HEADS, features // HEADS), 2, 0)


def heads_last(values_in):
    head_count, seq_count, positions, head_size = values_in.shape
    return jnp.moveaxis(values_in, 0, 2).reshape(seq_count, positions, head_count * head_size)


def column_sum(values_in):
    return jnp.sum(values_in.astype(jnp.float32), axis=0)


def on_device(
    tokens,
    lengths,
    cotangent,
    query_weight,
    query_bias,
    key_matrix,
    value_weight,
    value_bias,
    output_weight,
    output_bias,
    attn_gain,
    attn_shift,
    up_weight,
    up_bias,
    down_weight,
    down_bias,
    ffn_gain,
    ffn_shift,
):
    seq_count, seq_rows, features = tokens.shape
    key_total = seq_rows * lax.axis_size("blk")
    score_scale = 1.0 / math.sqrt(features // HEADS)
    flat_tokens = tokens.reshape(seq_count * seq_rows, features)
    counted = jnp.arange(key_total, dtype=jnp.int32)[None, None, :] < lengths[:, None, None]
    queries = (
        jnp.dot(flat_tokens, query_weight, preferred_element_type=jnp.float32) + query_bias
    ).astype(jnp.bfloat16)
    keyset = jnp.dot(flat_tokens, key_matrix, preferred_element_type=jnp.float32).astype(
        jnp.bfloat16
    )
    valset = (
        jnp.dot(flat_tokens, value_weight, preferred_element_type=jnp.float32) + value_bias
    ).astype(jnp.bfloat16)
    own_keys = keyset.reshape(seq_count, seq_rows, features)
    own_values = valset.reshape(seq_count, seq_rows, features)
    keys_all, values_all = (
        lax.all_gather(own_keys, "blk", axis=1, tiled=True),
        lax.all_gather(own_values, "blk", axis=1, tiled=True),
    )
    query_seq = queries.reshape(seq_count, seq_rows, features)
    query_heads = heads_first(query_seq)
    key_heads = heads_first(keys_all)
    value_heads = heads_first(values_all)

    def forward_head(pieces):
        single_query_head, single_key_head, single_value_head = pieces
        scores = (
            jnp.einsum(
                "pne,pme->pnm",
                single_query_head,
                single_key_head,
                preferred_element_type=jnp.float32,
            )
            * score_scale
        )
        masked = jnp.where(counted, scores, -1e30)
        largest = jnp.max(masked, axis=-1, keepdims=True)
        raised = jnp.exp(masked - largest)
        row_total = jnp.sum(raised, axis=-1, keepdims=True)
        reduced_probabilities = (raised / row_total).astype(jnp.bfloat16)
        mixed_head = jnp.einsum(
            "ocp,opn->ocn",
            reduced_probabilities,
            single_value_head,
            preferred_element_type=jnp.float32,
        )
        return (mixed_head.astype(jnp.bfloat16), (largest + jnp.log(row_total))[..., 0])

    mixed_heads, lse_heads = lax.map(forward_head, (query_heads, key_heads, value_heads))
    mixed_out = heads_last(mixed_heads).reshape(seq_count * seq_rows, features)
    attended = jnp.dot(mixed_out, output_weight, preferred_element_type=jnp.float32) + output_bias
    first_sum = flat_tokens.astype(jnp.float32) + attended
    hidden, attn_pull = jax.vjp(norm_rows, first_sum, attn_gain, attn_shift)
    hidden_low = hidden.astype(jnp.bfloat16)
    inner_act = jnp.dot(hidden_low, up_weight, preferred_element_type=jnp.float32) + up_bias
    gelu_value, gelu_pull = jax.vjp(gelu_exact, inner_act)
    active = gelu_value.astype(jnp.bfloat16)
    ffn_out = jnp.dot(active, down_weight, preferred_element_type=jnp.float32) + down_bias
    normalized_rows, ffn_pull = jax.vjp(norm_rows, hidden + ffn_out, ffn_gain, ffn_shift)
    encoded = normalized_rows.astype(jnp.bfloat16).reshape(seq_count, seq_rows, features)
    g_second, fgain_part, fshift_part = ffn_pull(
        cotangent.reshape(seq_count * seq_rows, features).astype(jnp.float32)
    )
    g_ffn = g_second.astype(jnp.bfloat16)
    dweight_part = row_dot(active, g_ffn)
    dbias_part = column_sum(g_ffn)
    (g_inner_wide,) = gelu_pull(col_dot(g_ffn, down_weight))
    g_inner = g_inner_wide.astype(jnp.bfloat16)
    uweight_part = row_dot(hidden_low, g_inner)
    ubias_part = column_sum(g_inner)
    g_hidden = g_second + col_dot(g_inner, up_weight)
    g_first, again_part, ashift_part = attn_pull(g_hidden)
    g_att = g_first.astype(jnp.bfloat16)
    oweight_part = row_dot(mixed_out, g_att)
    obias_part = column_sum(g_att)
    g_mixed = col_dot(g_att, output_weight).astype(jnp.bfloat16)
    keys_back, values_back = (
        lax.all_gather(own_keys, "blk", axis=1, tiled=True),
        lax.all_gather(own_values, "blk", axis=1, tiled=True),
    )
    key_back_heads = heads_first(keys_back)
    value_back_heads = heads_first(values_back)
    g_mixed_seq = g_mixed.reshape(seq_count, seq_rows, features)
    grad_mixed_heads = heads_first(g_mixed_seq)

    def backward_head(pieces):
        single_query_head, single_key_head, single_value_head, lse_head, head_gradient = pieces
        scores = (
            jnp.einsum(
                "pne,pme->pnm",
                single_query_head,
                single_key_head,
                preferred_element_type=jnp.float32,
            )
            * score_scale
        )
        soft_probs = jnp.where(counted, jnp.exp(scores - lse_head[..., None]), 0.0)
        reduced_probabilities = soft_probs.astype(jnp.bfloat16)
        grad_value = jnp.einsum(
            "xwr,xwa->xra", reduced_probabilities, head_gradient, preferred_element_type=jnp.float32
        )
        grad_probs = jnp.einsum(
            "pne,pme->pnm", head_gradient, single_value_head, preferred_element_type=jnp.float32
        )
        row_inner = jnp.sum(soft_probs * grad_probs, axis=-1, keepdims=True)
        score_gradient = (soft_probs * (grad_probs - row_inner)).astype(jnp.bfloat16)
        grad_query = (
            jnp.einsum(
                "ocp,opn->ocn", score_gradient, single_key_head, preferred_element_type=jnp.float32
            )
            * score_scale
        )
        grad_key = (
            jnp.einsum(
                "xwr,xwa->xra",
                score_gradient,
                single_query_head,
                preferred_element_type=jnp.float32,
            )
            * score_scale
        )
        return (grad_query, grad_key, grad_value)

    query_grads, key_grads, value_grads = lax.map(
        backward_head, (query_heads, key_back_heads, value_back_heads, lse_heads, grad_mixed_heads)
    )
    key_grads_own, value_grads_own = (
        lax.psum_scatter(
            heads_last(key_grads).astype(jnp.bfloat16), "blk", scatter_dimension=1, tiled=True
        ).astype(jnp.float32),
        lax.psum_scatter(
            heads_last(value_grads).astype(jnp.bfloat16), "blk", scatter_dimension=1, tiled=True
        ).astype(jnp.float32),
    )
    g_query = heads_last(query_grads).reshape(seq_count * seq_rows, features).astype(jnp.bfloat16)
    g_key = key_grads_own.reshape(seq_count * seq_rows, features).astype(jnp.bfloat16)
    g_value = value_grads_own.reshape(seq_count * seq_rows, features).astype(jnp.bfloat16)
    qweight_part = row_dot(flat_tokens, g_query)
    qbias_part = column_sum(g_query)
    kweight_part = row_dot(flat_tokens, g_key)
    vweight_part = row_dot(flat_tokens, g_value)
    vbias_part = column_sum(g_value)
    token_wide = (
        g_first
        + col_dot(g_query, query_weight)
        + col_dot(g_key, key_matrix)
        + col_dot(g_value, value_weight)
    )
    token_grad = token_wide.astype(jnp.bfloat16).reshape(seq_count, seq_rows, features)
    qrow, krow, vrow, orow, urow, drow = (
        lax.psum_scatter(
            qweight_part.astype(jnp.bfloat16), "dp", scatter_dimension=0, tiled=True
        ).astype(jnp.float32),
        lax.psum_scatter(
            kweight_part.astype(jnp.bfloat16), "dp", scatter_dimension=0, tiled=True
        ).astype(jnp.float32),
        lax.psum_scatter(
            vweight_part.astype(jnp.bfloat16), "dp", scatter_dimension=0, tiled=True
        ).astype(jnp.float32),
        lax.psum_scatter(
            oweight_part.astype(jnp.bfloat16), "dp", scatter_dimension=0, tiled=True
        ).astype(jnp.float32),
        lax.psum_scatter(
            uweight_part.astype(jnp.bfloat16), "dp", scatter_dimension=0, tiled=True
        ).astype(jnp.float32),
        lax.psum_scatter(
            dweight_part.astype(jnp.bfloat16), "dp", scatter_dimension=0, tiled=True
        ).astype(jnp.float32),
    )
    qfinal, kfinal, vfinal, ofinal, ufinal, dfinal = (
        lax.psum(qrow.astype(jnp.bfloat16), "blk").astype(jnp.float32),
        lax.psum(krow.astype(jnp.bfloat16), "blk").astype(jnp.float32),
        lax.psum(vrow.astype(jnp.bfloat16), "blk").astype(jnp.float32),
        lax.psum(orow.astype(jnp.bfloat16), "blk").astype(jnp.float32),
        lax.psum(urow.astype(jnp.bfloat16), "blk").astype(jnp.float32),
        lax.psum(drow.astype(jnp.bfloat16), "blk").astype(jnp.float32),
    )
    (
        qbias_sum,
        vbias_sum,
        obias_sum,
        again_sum,
        ashift_sum,
        ubias_sum,
        dbias_sum,
        fgain_sum,
        fshift_sum,
    ) = lax.psum(
        (
            qbias_part,
            vbias_part,
            obias_part,
            again_part,
            ashift_part,
            ubias_part,
            dbias_part,
            fgain_part,
            fshift_part,
        ),
        ("dp", "blk"),
    )
    return (
        encoded,
        token_grad,
        qfinal,
        qbias_sum,
        kfinal,
        vfinal,
        vbias_sum,
        ofinal,
        obias_sum,
        again_sum,
        ashift_sum,
        ufinal,
        ubias_sum,
        dfinal,
        dbias_sum,
        fgain_sum,
        fshift_sum,
    )


def solution(mesh):
    return jax.shard_map(
        on_device_fused if dict(mesh.shape) == {"dp": 16, "blk": 2} else on_device,
        mesh=mesh,
        in_specs=(
            P("dp", "blk", None),
            P("dp"),
            P("dp", "blk", None),
            P(),
            P(),
            P(),
            P(),
            P(),
            P(),
            P(),
            P(),
            P(),
            P(),
            P(),
            P(),
            P(),
            P(),
            P(),
        ),
        out_specs=(
            P("dp", "blk", None),
            P("dp", "blk", None),
            P("dp", None),
            P(),
            P("dp", None),
            P("dp", None),
            P(),
            P("dp", None),
            P(),
            P(),
            P(),
            P("dp", None),
            P(),
            P("dp", None),
            P(),
            P(),
            P(),
        ),
        check_vma=False,
    )
```

```python
import math

import jax
import jax.numpy as jnp
from jax import lax
from jax.experimental import pallas as pl
from jax.experimental.pallas import tpu as pltpu
from jax.sharding import PartitionSpec as P

MESH = pl.DeviceIdType.MESH
f32, bf16 = jnp.float32, jnp.bfloat16

HEADS = 12
EPSILON = 1e-05

LOG2E = math.log2(math.e)
LN2 = math.log(2.0)
AX = {"zh": (3, 1), "zl": (2, 2), "y": (1, 3), "x": (0, 4)}
BITS = ("c", "x", "y", "zl", "zh")
AXES = {"x": "x", "y": "y", "z": "zl", "h": "zh"}
ROUTES = {
    "D0": "xyzh", "D1": "yxhz", "D2": "zxyh", "D3": "xyzh", "D4": "zxyh", "D5": "yxhz",
    "U0": "yxzh", "U1": "zxyh", "U2": "zyxh", "U3": "xyzh", "U4": "yxzh", "U5": "zyxh",
    "O0": "zhxy", "O1": "yxzh", "O2": "zxyh", "Q0": "yzxh", "K0": "xyzh", "V0": "yxzh",
    "Q1": "xyhz", "K1": "xyhz", "V1": "yxzh", "Q2": "zxyh", "K2": "yxzh", "V2": "xyzh",
}
PIECES = tuple((n, 96 if n[0] in "DU" else 48, 128) for n in ROUTES)
NAMES = [p[0] for p in PIECES]
N_PIECES = len(PIECES)
ROW_O, ROW_AGAIN, ROW_ASHIFT, ROW_U, ROW_D, ROW_FGAIN, ROW_FSHIFT = 2, 3, 4, 5, 9, 10, 11
ROW_Q, ROW_V = 16, 17


def bit(dp, ax):
    return lax.rem(lax.div(dp, 1 << AX[ax][0]), 2)


def peer_of(ax):
    dp, c = lax.axis_index("dp"), lax.axis_index("blk")
    if ax == "c":
        return (dp, 1 - c)
    return (dp + (1 - 2 * bit(dp, ax)) * (1 << AX[ax][0]), c)


def dot_nn(a, b):
    return jnp.dot(a, b, preferred_element_type=f32)


def dot_nt(a, b):
    return lax.dot_general(a, b, (((1,), (1,)), ((), ())), preferred_element_type=f32)


def dot_tn(a, b):
    return lax.dot_general(a, b, (((0,), (0,)), ((), ())), preferred_element_type=f32)


def fold8(v):
    return jnp.sum(v.reshape(v.shape[0] // 8, 8, v.shape[1]), axis=0)


class Piece:
    def __init__(self, idx, own, other, recvs, fin, ssem, rsem):
        self.name, self.R, self.C = PIECES[idx]
        self.idx, self.own, self.other, self.recvs, self.fin = idx, own, other, recvs, fin
        self.ssem, self.rsem = ssem, rsem
        self.order = [AXES[a] for a in ROUTES[self.name]]
        self.dp = lax.axis_index("dp")
        self.gone = set()

    def view(self, k, mine):
        idx = [slice(None)] * 4
        for j in range(k):
            ax = self.order[j]
            own = bit(self.dp, ax)
            idx[AX[ax][1] - 1] = own if (j < k - 1 or mine) else 1 - own
        return tuple(idx)

    def copy(self, k):
        if k == 0:
            src, ax = self.other, "c"
        else:
            src, ax = self.own.at[self.view(k, False)], self.order[k - 1]
        return pltpu.make_async_remote_copy(
            src, self.recvs[k], self.ssem.at[self.idx], self.rsem.at[self.idx, k], device_id=peer_of(ax), device_id_type=MESH
        )

    def start(self):
        self.copy(0).start()

    def sent(self, k):
        if k not in self.gone:
            self.copy(k).wait_send()
            self.gone.add(k)

    def finish(self, k):
        self.copy(k).wait_recv()
        self.sent(k)
        v = self.view(k, True)
        total = self.own[v].astype(f32) + self.recvs[k][...].astype(f32)
        if k < 4:
            self.own[v] = total.astype(bf16)
            self.copy(k + 1).start()
        else:
            self.fin[...] = total


class Vector:
    def __init__(self, idx, acc, recv, ssem, rsem):
        self.idx, self.acc, self.recv, self.ssem, self.rsem = idx, acc, recv, ssem, rsem

    def copy(self, k):
        return pltpu.make_async_remote_copy(
            self.acc.at[k], self.recv.at[k], self.ssem.at[self.idx], self.rsem.at[self.idx, k],
            device_id=peer_of(BITS[k]), device_id_type=MESH,
        )

    def start(self, k):
        self.copy(k).start()

    def step(self, k):
        self.copy(k).wait()
        self.acc[k + 1] = self.acc[k] + self.recv[k]
        if k < 4:
            self.start(k + 1)


def layer_kernel(*refs):
    (tok_h, len_s, cot_h, wq_h, bq, wk_h, wv_h, bv, wo_h, bo, g1, b1, wu_h, bu, wd_h, bd, g2, b2) = refs[:18]
    enc_o, tg_o, du_o, small_o, vec_o, e_hbm = refs[18:24]
    (X, WU, WD, WO, Q, KO, KP, VO, VP, MB, MIX, LINV, T1, T2, T3, RSTD, HL, G, DO, CD, FAB, KR, VR,
     DU, SB, RDU, RS, SDU, SS, FDU, FS, b_acc, b_recv, l_acc, l_recv,
     VEC, LEN, wsem, vsem, esem, osem, ksem_s, ksem_r, ssem, rsem, fsem_s, fsem_r) = refs[24:]
    c = lax.axis_index("blk")
    rows = X.shape[0]
    D = X.shape[1]
    scale = 1.0 / math.sqrt(D // HEADS)

    def load(src, dst, sem):
        cp = pltpu.make_async_copy(src, dst, sem)
        cp.start()
        return cp

    ld_x = load(tok_h.at[0], X, wsem.at[5])
    ld_k = load(wk_h, WU.at[:, pl.ds(0, D)], wsem.at[0])
    vec_in = (bq, bv, bo, g1, b1, bd, g2, b2, bu)
    ld_vec = [load(v, dst, vsem.at[i]) for i, (v, dst) in enumerate(zip(vec_in, VEC))]
    ld_len = load(len_s, LEN, vsem.at[9])
    ld_v = load(wv_h, WU.at[:, pl.ds(D, D)], wsem.at[1])
    ld_q = load(wq_h, WU.at[:, pl.ds(2 * D, D)], wsem.at[2])

    barrier = pltpu.get_barrier_semaphore()
    for ax in BITS:
        pl.semaphore_signal(barrier, inc=1, device_id=peer_of(ax), device_id_type=MESH)

    def pick(half, mine, theirs):
        return jnp.where(half == c, mine, theirs)

    pieces = {}
    for i, name in enumerate(NAMES):
        if i < 12:
            own, other, recvs, fin = DU.at[i], DU.at[12 + i % 6], [r.at[i] for r in (RDU,) + SDU], FDU.at[i, c]
        else:
            k = i - 12
            own, other, recvs, fin = SB.at[k], SB.at[12 + k % 3], [r.at[k] for r in (RS,) + SS], FS.at[k, c]
        pieces[name] = Piece(i, own, other, recvs, fin, ssem, rsem)

    def step(label):
        for name, k in HOOKS.get(label, ()):
            if name == "early":
                early.step(k)
            elif name == "late":
                late.step(k)
            else:
                pieces[name].finish(k)
                if k == 4:
                    group = min(NAMES.index(name) // 6, 2)
                    left[group] -= 1
                    if not left[group]:
                        last_copy(group).start()

    left = [6, 6, 12]

    def last_copy(g):
        ref = (FDU.at[pl.ds(0, 6), c], FDU.at[pl.ds(6, 6), c], FS.at[:, c])[g]
        return pltpu.make_async_remote_copy(
            ref, ref, fsem_s.at[g], fsem_r.at[g], device_id=peer_of("c"), device_id_type=MESH
        )

    early = Vector(N_PIECES, b_acc, b_recv, ssem, rsem)
    late = Vector(N_PIECES + 1, l_acc, l_recv, ssem, rsem)
    b_acc[0] = jnp.zeros(b_acc.shape[1:], f32)

    lane = lax.broadcasted_iota(jnp.int32, (rows, 128), 1)
    low = lane < 64
    ld_len.wait()
    length = LEN[0]
    pos = lax.broadcasted_iota(jnp.int32, (rows, 128), 0)
    MB[0] = jnp.where(pos + c * rows < length, 0.0, -1e30).astype(bf16)
    MB[1] = jnp.where(pos + (1 - c) * rows < length, 0.0, -1e30).astype(bf16)

    def kv_send(src, dst, i):
        cp = pltpu.make_async_remote_copy(
            src.at[:, pl.ds(384 * (i % 2), 384)], dst.at[:, pl.ds(384 * (i % 2), 384)], ksem_s.at[6 + i], ksem_r.at[6 + i],
            device_id=peer_of("c"), device_id_type=MESH,
        )
        cp.start()
        return cp

    ld_x.wait()
    ld_k.wait()
    KO[...] = dot_nn(X[...], WU[:, :D]).astype(bf16)
    pl.semaphore_wait(barrier, 5)
    kv = [kv_send(KO, KP, 0)]
    ld_o = load(wo_h, WO, wsem.at[4])
    ld_c = load(cot_h.at[0], CD, wsem.at[6])
    for cp in ld_vec:
        cp.wait()
    bq, bv, bo, g1, b1, bd, g2, b2, bu = (v[...].reshape(1, -1) for v in VEC)
    ld_v.wait()
    VO[...] = (dot_nn(X[...], WU[:, D : 2 * D]) + bv).astype(bf16)
    kv += [kv_send(VO, VP, 2), kv_send(KO, KP, 1), kv_send(VO, VP, 3)]
    FFC = 512
    ld_q.wait()
    Q[...] = ((dot_nn(X[...], WU[:, 2 * D : 3 * D]) + bq) * (scale * LOG2E)).astype(bf16)
    ld_u = load(wu_h, WU, wsem.at[3])
    ld_d = load(wd_h, WD, wsem.at[1])

    one, zero = jnp.ones((rows, 128), bf16), jnp.zeros((rows, 128), bf16)
    hot = [jnp.where(lane == 64, 1.0, 0.0).astype(bf16), jnp.where(lane == 0, 1.0, 0.0).astype(bf16)]

    def own_lanes(j, mine, rest):
        return jnp.where(low, mine, rest) if j == 0 else jnp.where(low, rest, mine)

    def e_slot(row, h, n, sem, out):
        buf, far = FAB.at[pl.ds(row, 1024 * n), :], e_hbm.at[pl.ds(1024 * h, 1024 * n), :]
        return pltpu.make_async_copy(buf, far, sem) if out else pltpu.make_async_copy(far, buf, sem)

    def e_out(g):
        return e_slot(3072 * (g % 2), 3 * g, 3, esem.at[g % 2], True)

    res = []
    for h in range(HEADS):
        p, j = divmod(h, 2)
        g = h // 3
        ls = slice(128 * p, 128 * p + 128)
        if h == 0:
            kv[0].wait_recv()
            kv[1].wait_recv()
        if h == 6:
            kv[2].wait_recv()
            kv[3].wait_recv()
        if h % 3 == 0 and g >= 2:
            e_out(g - 2).wait()
        q = own_lanes(j, Q[:, ls], hot[j])
        s_o = dot_nt(q, own_lanes(j, KO[:, ls], MB[0]))
        s_p = dot_nt(q, own_lanes(j, KP[:, ls], MB[1]))
        m = jnp.maximum(jnp.max(s_o, axis=1, keepdims=True), jnp.max(s_p, axis=1, keepdims=True))
        e_o = jnp.exp2(s_o - m).astype(bf16)
        e_p = jnp.exp2(s_p - m).astype(bf16)
        base = 1024 * (h % 6)
        FAB[base : base + 512, :] = e_o
        FAB[base + 512 : base + 1024, :] = e_p
        res.append(dot_nn(e_o, own_lanes(j, VO[:, ls], one)) + dot_nn(e_p, own_lanes(j, VP[:, ls], one)))
        if j == 1:
            inv = 1.0 / pltpu.roll(jnp.where(low, res[1], res[0]), 64, 1)
            MIX[:, ls] = (jnp.where(low, res[0], res[1]) * inv).astype(bf16)
            LINV[:, ls] = inv
            res = []
        if h % 3 == 2:
            e_out(g).start()

    ld_o.wait()
    T2[...] = dot_nn(MIX[...], WO[...])
    BR = 128
    for r in range(0, rows, BR):
        rs = slice(r, r + BR)
        r1 = X[rs, :].astype(f32) + (T2[rs, :] + bo)
        cen = r1 - jnp.mean(r1, axis=1, keepdims=True)
        rstd = lax.rsqrt(jnp.mean(cen * cen, axis=1, keepdims=True) + EPSILON)
        xh = cen * rstd
        T1[rs, :] = xh
        RSTD[rs, :] = rstd
        HL[rs, :] = (xh * g1 + b1).astype(bf16)
    e_out(2).wait()
    e_out(3).wait()

    ld_u.wait()
    ld_d.wait()
    for j in range(6):
        u = dot_nn(HL[...], WU[:, FFC * j : FFC * j + FFC]) + bu[:, FFC * j : FFC * j + FFC]
        half = 0.5 * (1.0 + lax.erf(u * (1.0 / math.sqrt(2.0))))
        act = (u * half).astype(bf16)
        FAB[512 * j : 512 * j + 512, :] = act
        slope = half + u * (jnp.exp(u * u * -0.5) * (1.0 / math.sqrt(2.0 * math.pi)))
        FAB[3072 + 512 * j : 3072 + 512 * j + 512, :] = slope.astype(bf16)
        y = dot_nn(act, WD[FFC * j : FFC * j + FFC, :])
        T2[...] = y if j == 0 else T2[...] + y

    ld_c.wait()
    sums = [jnp.zeros((8, D), f32)] * 3
    for r in range(0, rows, BR):
        rs = slice(r, r + BR)
        r2 = (T1[rs, :] * g1 + b1) + (T2[rs, :] + bd)
        cen = r2 - jnp.mean(r2, axis=1, keepdims=True)
        rstd = lax.rsqrt(jnp.mean(cen * cen, axis=1, keepdims=True) + EPSILON)
        xh = cen * rstd
        DO[rs, :] = (xh * g2 + b2).astype(bf16)
        dy = CD[rs, :].astype(f32)
        dx = dy * g2
        g = rstd * (dx - jnp.mean(dx, axis=1, keepdims=True) - xh * jnp.mean(dx * xh, axis=1, keepdims=True))
        T2[rs, :] = g
        gl = g.astype(bf16)
        G[rs, :] = gl
        sums = [sums[0] + fold8(dy * xh), sums[1] + fold8(dy), sums[2] + fold8(gl.astype(f32))]
    enc_copy = load(DO, enc_o.at[0], osem.at[0])
    for row, s in zip((ROW_FGAIN, ROW_FSHIFT, ROW_D), sums):
        b_acc[0, row : row + 1, :] = jnp.sum(s, axis=0, keepdims=True)

    for t in range(3):
        for j in range(6):
            w = dot_tn(FAB[512 * j : 512 * j + 512, :], G[:, 256 * t : 256 * t + 256]).astype(bf16)
            at = 512 * j
            while at < 512 * j + 512:
                seg, off = divmod(at, 96)
                size = min(96 - off, 512 * j + 512 - at)
                i, half = divmod(seg, 2)
                for u in range(2):
                    where = (pick(half, 2 * t + u, 12 + 2 * t + u), i // 8, (i // 4) % 2, (i // 2) % 2, i % 2)
                    DU[where + (slice(off, off + size),)] = w[at - 512 * j : at - 512 * j + size, 128 * u : 128 * u + 128]
                at += size
        pieces["D%d" % (2 * t)].start()
        pieces["D%d" % (2 * t + 1)].start()
        step("D%d" % t)

    def e_in(h):
        slot = h % 4
        return e_slot((0, 1024, 2048, 6144)[slot], h, 1, esem.at[slot], False)

    for h in range(4):
        e_in(h).start()

    for n, j in enumerate((0, 3, 1, 4, 2, 5)):
        hf, t = divmod(j, 3)
        frow = slice(3072 + 512 * j, 3072 + 512 * j + 512)
        gi32 = dot_nt(G[...], WD[FFC * j : FFC * j + FFC, :]) * FAB[frow, :].astype(f32)
        gi = gi32.astype(bf16)
        step("G%d" % n)
        FAB[frow, :] = gi
        s = jnp.sum(fold8(gi.astype(f32)), axis=0, keepdims=True)
        at = 512 * j
        while at < 512 * j + 512:
            row, off = divmod(at, D)
            size = min(D - off, 512 * j + 512 - at)
            b_acc[0, ROW_U + row : ROW_U + row + 1, off : off + size] = s[:, at - 512 * j : at - 512 * j + size]
            at += size
        w = dot_tn(HL[...], gi).astype(bf16)
        if hf == 0:
            pieces["D%d" % (2 * t)].sent(0)
            pieces["D%d" % (2 * t + 1)].sent(0)
        for u in range(2):
            dst = pick(hf, 6 + 2 * t + u, 12 + 2 * t + u)
            for i in range(16):
                where = (dst, i // 8, (i // 4) % 2, (i // 2) % 2, i % 2)
                for v in range(2):
                    col = 256 * u + 128 * v
                    DU[where + (slice(48 * v, 48 * v + 48),)] = w[48 * i : 48 * i + 48, col : col + 128]
        y = dot_nt(gi, WU[:, FFC * j : FFC * j + FFC])
        T3[...] = (T2[...] if n == 0 else T3[...]) + y
        if hf == 1:
            pieces["U%d" % (2 * t)].start()
            pieces["U%d" % (2 * t + 1)].start()
        step("F%d" % n)

    ld_q = load(wq_h, WU.at[:, pl.ds(0, D)], wsem.at[0])
    ld_k = load(wk_h, WU.at[:, pl.ds(D, D)], wsem.at[1])
    ld_v = load(wv_h, WU.at[:, pl.ds(2 * D, D)], wsem.at[2])

    sums = [jnp.zeros((8, D), f32)] * 3
    for r in range(0, rows, BR):
        rs = slice(r, r + BR)
        gh = T3[rs, :]
        xh = T1[rs, :]
        dx = gh * g1
        g = RSTD[rs, :] * (dx - jnp.mean(dx, axis=1, keepdims=True) - xh * jnp.mean(dx * xh, axis=1, keepdims=True))
        T3[rs, :] = g
        gl = g.astype(bf16)
        G[rs, :] = gl
        sums = [sums[0] + fold8(gh * xh), sums[1] + fold8(gh), sums[2] + fold8(gl.astype(f32))]
    for row, s in zip((ROW_AGAIN, ROW_ASHIFT, ROW_O), sums):
        b_acc[0, row : row + 1, :] = jnp.sum(s, axis=0, keepdims=True)
    early.start(0)
    step("N")

    w = dot_tn(MIX[...], G[...]).astype(bf16)
    for half in range(2):
        for t in range(3):
            at = 384 * half + 128 * t
            SB[pick(half, t, 12 + t)] = w[:, at : at + 128].reshape(2, 2, 2, 2, 48, 128)
    for t in range(3):
        pieces["O%d" % t].start()
    step("M")
    enc_copy.wait()
    DO[...] = dot_nt(G[...], WO[...]).astype(bf16)

    step("P")

    def projection(m, t, grad):
        pieces[NAMES[12 + 3 * t + m]].sent(0)
        w = dot_tn(X[...], grad).astype(bf16)
        for half in range(2):
            SB[pick(half, 3 + 3 * t + m, 12 + m)] = w[:, 128 * half : 128 * half + 128].reshape(2, 2, 2, 2, 48, 128)

    def key_value(t):
        cs = slice(256 * t, 256 * t + 256)
        HL[:, cs] = (FAB[KT + 256 * t : KT + 256 * t + 256, :].astype(f32) + KR[cs, :].astype(f32)).astype(bf16).T
        projection(1, t, HL[:, cs])
        G[:, cs] = (FAB[VT + 256 * t : VT + 256 * t + 256, :].astype(f32) + VR[cs, :].astype(f32)).astype(bf16).T
        projection(2, t, G[:, cs])

    KT, KTP, VT, VTP = 3072, 3072 + D, 3072 + 2 * D, 3072 + 3 * D
    back = []
    for p in range(HEADS // 2):
        ls = slice(128 * p, 128 * p + 128)
        ps = 128 * p
        dos = DO[:, ls].astype(f32) * LINV[:, ls]
        extra = pltpu.roll(dos * MIX[:, ls].astype(f32), 64, 1) * -1.0
        dos = dos.astype(bf16)
        extra = extra.astype(bf16)
        dos_t = dos.T
        q_t = Q[:, ls].T
        dq = []
        e_in(2 * p).wait()
        e_in(2 * p + 1).wait()
        t = p // 2
        if p in (3, 5):
            back[2 * t - 2].wait_recv()
            back[2 * t - 1].wait_recv()
        for j in range(2):
            h = 2 * p + j
            base = (0, 1024, 2048, 6144)[h % 4]
            d_ext = own_lanes(j, dos, extra)
            rt = slice(64 * j, 64 * j + 64)
            acc = None
            for half, (k, v, kt, vt) in enumerate(((KO, VO, KT, VT), (KP, VP, KTP, VTP))):
                e = FAB[base + 512 * half : base + 512 * half + 512, :]
                dp = dot_nt(d_ext, own_lanes(j, v[:, ls], one))
                ds = (e.astype(f32) * dp).astype(bf16)
                x = dot_nn(ds, k[:, ls])
                acc = x if acc is None else acc + x
                FAB[vt + ps + 64 * j : vt + ps + 64 * j + 64, :] = dot_nn(dos_t[rt], e).astype(bf16)
                FAB[kt + ps + 64 * j : kt + ps + 64 * j + 64, :] = (dot_nn(q_t[rt], ds) * LN2).astype(bf16)
            dq.append(acc)
        CD[:, ls] = (jnp.where(low, dq[0], dq[1]) * scale).astype(bf16)
        if p % 2 == 1:
            projection(0, t, CD[:, 256 * t : 256 * t + 256])
        if p in (3, 5):
            key_value(t - 1)
        if p + 2 < HEADS // 2:
            e_in(2 * p + 4).start()
            e_in(2 * p + 5).start()
        if p % 2 == 1:
            for i, (src, dst) in enumerate(((KTP, KR), (VTP, VR))):
                cp = pltpu.make_async_remote_copy(
                    FAB.at[pl.ds(src + 256 * t, 256), :], dst.at[pl.ds(256 * t, 256), :],
                    ksem_s.at[2 * t + i], ksem_r.at[2 * t + i], device_id=peer_of("c"), device_id_type=MESH,
                )
                cp.start()
                back.append(cp)
            pieces["Q%d" % t].start()
        if p in (3, 5):
            pieces["K%d" % (t - 1)].start()
            pieces["V%d" % (t - 1)].start()
        step("H%d" % p)

    ld_q.wait()
    ld_k.wait()
    ld_v.wait()
    T3[...] += dot_nt(CD[...], WU[:, :D])
    late.acc[0, 0:1, :] = jnp.sum(fold8(CD[...].astype(f32)), axis=0, keepdims=True)
    late.acc[0, 2:8, :] = jnp.zeros((6, D), f32)
    back[4].wait_recv()
    back[5].wait_recv()
    key_value(2)
    late.acc[0, 1:2, :] = jnp.sum(fold8(G[...].astype(f32)), axis=0, keepdims=True)
    pieces["K2"].start()
    pieces["V2"].start()
    late.start(0)
    step("V")
    MIX[...] = (T3[...] + dot_nt(HL[...], WU[:, D : 2 * D]) + dot_nt(G[...], WU[:, 2 * D : 3 * D])).astype(bf16)
    tg_copy = load(MIX, tg_o.at[0], osem.at[1])

    step("T")
    vec_copies = [load(early.acc.at[5], vec_o.at[pl.ds(0, 16)], osem.at[2])]
    vec_copies.append(load(late.acc.at[5], vec_o.at[pl.ds(16, 8)], osem.at[3]))

    outs = []
    for g in range(3):
        last_copy(g).wait_recv()
    outs = [load(FDU, du_o, osem.at[4]), load(FS, small_o, osem.at[5])]
    for cp in outs:
        cp.wait()
    for cp in vec_copies:
        cp.wait()
    tg_copy.wait()
    for cp in kv + back:
        cp.wait_send()
    for g in range(3):
        last_copy(g).wait_send()


HOOKS = {
    "D2": (("D0", 0), ("D1", 0),),
    "G0": (("D2", 0), ("D3", 0), ("D4", 0), ("D5", 0),),
    "F3": (("U0", 0), ("U1", 0),),
    "F4": (("D1", 1), ("D0", 1), ("U2", 0), ("U3", 0), ("D3", 1), ("D5", 1), ("D2", 1),),
    "F5": (("D4", 1),),
    "P": (("U4", 0), ("U5", 0), ("early", 0),),
    "H0": (("O0", 0), ("O1", 0), ("O2", 0), ("U1", 1), ("U0", 1),),
    "H1": (("D0", 2), ("D3", 2), ("U2", 1), ("D1", 2),),
    "H2": (("Q0", 0),),
    "H3": (("D5", 2), ("D2", 2), ("early", 1), ("O1", 1), ("U4", 1), ("D4", 2),),
    "H4": (("U2", 2), ("K0", 0), ("Q1", 0), ("V0", 0), ("Q0", 1), ("D0", 3), ("D3", 3), ("U1", 2), ("O0", 1),
        ("U0", 2), ("D1", 3), ("O2", 1),),
    "H5": (("U3", 1), ("U5", 1), ("D5", 3), ("D2", 3), ("early", 2), ("O1", 2), ("D4", 3),),
    "V": (("U1", 3), ("K1", 0), ("Q2", 0), ("V1", 0), ("D0", 4), ("D3", 4), ("V0", 1), ("D1", 4),),
    "T": (("U2", 3), ("late", 0), ("K2", 0), ("V2", 0), ("U4", 2), ("Q0", 2), ("O2", 2), ("O0", 2), ("U0", 3),
        ("D5", 4), ("D2", 4), ("O1", 3), ("D4", 4), ("K0", 1), ("Q1", 1), ("U3", 2), ("U1", 4), ("U5", 2), ("O2", 3),
        ("U2", 4), ("early", 3), ("late", 1), ("Q0", 3), ("U0", 4), ("O1", 4), ("O0", 3), ("V0", 2), ("U4", 3),
        ("O2", 4), ("V1", 1), ("K1", 1), ("U5", 3), ("Q0", 4), ("V2", 1), ("K0", 2), ("O0", 4), ("U3", 3), ("Q1", 2),
        ("late", 2), ("K2", 1), ("Q2", 1), ("V0", 3), ("V1", 2), ("U4", 4), ("early", 4), ("K1", 2), ("V2", 2),
        ("K2", 2), ("U5", 4), ("Q2", 2), ("K0", 3), ("V0", 4), ("late", 3), ("U3", 4), ("Q1", 3), ("V1", 3),
        ("K1", 3), ("V2", 3), ("Q2", 3), ("K2", 3), ("K0", 4), ("Q1", 4), ("late", 4), ("V1", 4), ("K1", 4),
        ("V2", 4), ("Q2", 4), ("K2", 4),),
}


def layer_call(tokens, lengths, cotangent, wq, bq, wk, wv, bv, wo, bo, g1, b1, wu, bu, wd, bd, g2, b2):
    rows, D = tokens.shape[1:]
    lead = (2, 2, 2, 2)

    def ladder(n, R, C):
        return tuple(pltpu.VMEM((n,) + (2,) * (4 - k) + (R, C), bf16) for k in range(1, 5))

    big = pltpu.VMEM((rows, D), f32)
    low = pltpu.VMEM((rows, D), bf16)
    wide = pltpu.VMEM((D, D), bf16)
    scratch = [
        low, pltpu.VMEM((D, 4 * D), bf16), pltpu.VMEM((4 * D, D), bf16), wide, low, low, low, low, low, pltpu.VMEM((2, rows, 128), bf16), low, big,
        big, big, big, pltpu.VMEM((rows, 1), f32), low, low, low, low, pltpu.VMEM((7168, 512), bf16),
        pltpu.VMEM((D, rows), bf16), pltpu.VMEM((D, rows), bf16),
        pltpu.VMEM((18,) + lead + (96, 128), bf16), pltpu.VMEM((15,) + lead + (48, 128), bf16),
        pltpu.VMEM((12,) + lead + (96, 128), bf16), pltpu.VMEM((12,) + lead + (48, 128), bf16),
        ladder(12, 96, 128), ladder(12, 48, 128),
        pltpu.VMEM((12, 2, 96, 128), f32), pltpu.VMEM((12, 2, 48, 128), f32),
        pltpu.VMEM((6, 16, D), f32), pltpu.VMEM((5, 16, D), f32), pltpu.VMEM((6, 8, D), f32), pltpu.VMEM((5, 8, D), f32),
        (pltpu.VMEM((D,), f32),) * 8 + (pltpu.VMEM((4 * D,), f32),), pltpu.SMEM((1,), jnp.int32),
        pltpu.SemaphoreType.DMA((7,)), pltpu.SemaphoreType.DMA((10,)), pltpu.SemaphoreType.DMA((4,)),
        pltpu.SemaphoreType.DMA((6,)), pltpu.SemaphoreType.DMA((10,)), pltpu.SemaphoreType.DMA((10,)),
        pltpu.SemaphoreType.DMA((N_PIECES + 2,)), pltpu.SemaphoreType.DMA((N_PIECES + 2, 5)),
        pltpu.SemaphoreType.DMA((3,)), pltpu.SemaphoreType.DMA((3,)),
    ]
    hbm = pl.BlockSpec(memory_space=pl.ANY)
    sds = jax.ShapeDtypeStruct
    shapes = [sds(tokens.shape, bf16), sds(tokens.shape, bf16), sds((12, 2, 96, 128), f32), sds((12, 2, 48, 128), f32),
              sds((24, D), f32), sds((HEADS * 1024, 512), bf16)]
    return pl.pallas_call(
        layer_kernel,
        out_shape=shapes,
        in_specs=[hbm] * 18,
        out_specs=[hbm] * len(shapes),
        scratch_shapes=scratch,
        compiler_params=pltpu.CompilerParams(collective_id=0, has_side_effects=True, vmem_limit_bytes=VMEM_LIMIT),
    )(tokens, lengths, cotangent, wq, bq, wk, wv, bv, wo, bo, g1, b1, wu, bu, wd, bd,
      g2, b2)


VMEM_LIMIT = 64 << 20


def hand_on_kernel(enc, tg, du, small, vec, *refs):
    outs, vecs = refs[:8], refs[8 : 8 + len(VEC_ROWS)]
    stage, done, sem = refs[8 + len(VEC_ROWS) : -7], refs[-7:-1], refs[-1]
    ins = [pltpu.make_async_copy(r, s, sem.at[i]) for i, (r, s) in enumerate(zip((enc, tg, du, small, vec), stage))]
    for cp in ins:
        cp.start()
    back = [pltpu.make_async_copy(s, o, sem.at[5 + i]) for i, (s, o) in enumerate(zip(stage[:2] + done, outs))]
    for i in range(2):
        ins[i].wait()
        back[i].start()
    q, k, v, o, u, d = done
    ins[2].wait()
    for t in range(6):
        for half in range(2):
            d[96 * half : 96 * half + 96, 128 * t : 128 * t + 128] = stage[2][t, half]
            for w in range(2):
                col = 1536 * half + 256 * t + 128 * w
                u[:, col : col + 128] = stage[2][6 + t, half, 48 * w : 48 * w + 48]
    back[7].start()
    back[6].start()
    ins[3].wait()
    for t in range(3):
        for half in range(2):
            o[:, 384 * half + 128 * t : 384 * half + 128 * t + 128] = stage[3][t, half]
            for m, w in enumerate((q, k, v)):
                w[:, 128 * half + 256 * t : 128 * half + 256 * t + 128] = stage[3][3 + 3 * t + m, half]
    for i in range(2, 6):
        back[i].start()
    ins[4].wait()
    for ref, (row, count) in zip(vecs, VEC_ROWS):
        for k in range(count):
            ref[768 * k : 768 * k + 768] = stage[4][row + k]
    for cp in back:
        cp.wait()


VEC_ROWS = ((ROW_Q, 1), (ROW_V, 1), (ROW_O, 1), (ROW_AGAIN, 1), (ROW_ASHIFT, 1), (ROW_U, 4), (ROW_D, 1), (ROW_FGAIN, 1),
            (ROW_FSHIFT, 1))


def hand_on(arrays):
    hbm = pl.BlockSpec(memory_space=pl.ANY)
    vm = pl.BlockSpec(memory_space=pltpu.VMEM)
    shapes = [(a.shape, a.dtype) for a in arrays[:2]] + [((48, 768), f32)] * 4 + [((48, 3072), f32), ((192, 768), f32)]
    return pl.pallas_call(
        hand_on_kernel,
        out_shape=[jax.ShapeDtypeStruct(*a) for a in shapes] + [jax.ShapeDtypeStruct((768 * k,), f32) for _, k in VEC_ROWS],
        in_specs=[hbm] * 5,
        out_specs=[hbm] * 8 + [vm] * len(VEC_ROWS),
        scratch_shapes=[pltpu.VMEM(a.shape, a.dtype) for a in arrays] + [pltpu.VMEM(*a) for a in shapes[2:]]
        + [pltpu.SemaphoreType.DMA((13,))],
        compiler_params=pltpu.CompilerParams(vmem_limit_bytes=VMEM_LIMIT),
    )(*arrays)


def on_device_fused(*args):
    (enc, tg, qg, kg, vg, og, ug, dg, qb, vb, ob, ag, ash, ub, db, fg, fs) = hand_on(layer_call(*args)[:5])
    return (enc, tg, qg, qb, kg, vg, vb, og, ob, ag, ash, ug, ub, dg, db, fg, fs)


CONTRACT_ROWS = (((0,), (0,)), ((), ()))
CONTRACT_COLS = (((1,), (1,)), ((), ()))


def norm_rows(values_in, gain_vec, shift_vec):
    row_mean = jnp.mean(values_in, axis=-1, keepdims=True)
    centred = values_in - row_mean
    spread = jnp.mean(centred * centred, axis=-1, keepdims=True)
    return centred * lax.rsqrt(spread + EPSILON) * gain_vec + shift_vec


def gelu_exact(values_in):
    return 0.5 * values_in * (1.0 + lax.erf(values_in * (1.0 / math.sqrt(2.0))))


def row_dot(left, right):
    return lax.dot_general(left, right, CONTRACT_ROWS, preferred_element_type=jnp.float32)


def col_dot(left, right):
    return lax.dot_general(left, right, CONTRACT_COLS, preferred_element_type=jnp.float32)


def heads_first(values_in):
    seq_count, positions, features = values_in.shape
    return jnp.moveaxis(values_in.reshape(seq_count, positions, HEADS, features // HEADS), 2, 0)


def heads_last(values_in):
    head_count, seq_count, positions, head_size = values_in.shape
    return jnp.moveaxis(values_in, 0, 2).reshape(seq_count, positions, head_count * head_size)


def column_sum(values_in):
    return jnp.sum(values_in.astype(jnp.float32), axis=0)


def on_device(
    tokens,
    lengths,
    cotangent,
    query_weight,
    query_bias,
    key_matrix,
    value_weight,
    value_bias,
    output_weight,
    output_bias,
    attn_gain,
    attn_shift,
    up_weight,
    up_bias,
    down_weight,
    down_bias,
    ffn_gain,
    ffn_shift,
):
    seq_count, seq_rows, features = tokens.shape
    key_total = seq_rows * lax.axis_size("blk")
    score_scale = 1.0 / math.sqrt(features // HEADS)
    flat_tokens = tokens.reshape(seq_count * seq_rows, features)
    counted = jnp.arange(key_total, dtype=jnp.int32)[None, None, :] < lengths[:, None, None]
    queries = (
        jnp.dot(flat_tokens, query_weight, preferred_element_type=jnp.float32) + query_bias
    ).astype(jnp.bfloat16)
    keyset = jnp.dot(flat_tokens, key_matrix, preferred_element_type=jnp.float32).astype(
        jnp.bfloat16
    )
    valset = (
        jnp.dot(flat_tokens, value_weight, preferred_element_type=jnp.float32) + value_bias
    ).astype(jnp.bfloat16)
    own_keys = keyset.reshape(seq_count, seq_rows, features)
    own_values = valset.reshape(seq_count, seq_rows, features)
    keys_all, values_all = (
        lax.all_gather(own_keys, "blk", axis=1, tiled=True),
        lax.all_gather(own_values, "blk", axis=1, tiled=True),
    )
    query_seq = queries.reshape(seq_count, seq_rows, features)
    query_heads = heads_first(query_seq)
    key_heads = heads_first(keys_all)
    value_heads = heads_first(values_all)

    def forward_head(pieces):
        single_query_head, single_key_head, single_value_head = pieces
        scores = (
            jnp.einsum(
                "pne,pme->pnm",
                single_query_head,
                single_key_head,
                preferred_element_type=jnp.float32,
            )
            * score_scale
        )
        masked = jnp.where(counted, scores, -1e30)
        largest = jnp.max(masked, axis=-1, keepdims=True)
        raised = jnp.exp(masked - largest)
        row_total = jnp.sum(raised, axis=-1, keepdims=True)
        reduced_probabilities = (raised / row_total).astype(jnp.bfloat16)
        mixed_head = jnp.einsum(
            "ocp,opn->ocn",
            reduced_probabilities,
            single_value_head,
            preferred_element_type=jnp.float32,
        )
        return (mixed_head.astype(jnp.bfloat16), (largest + jnp.log(row_total))[..., 0])

    mixed_heads, lse_heads = lax.map(forward_head, (query_heads, key_heads, value_heads))
    mixed_out = heads_last(mixed_heads).reshape(seq_count * seq_rows, features)
    attended = jnp.dot(mixed_out, output_weight, preferred_element_type=jnp.float32) + output_bias
    first_sum = flat_tokens.astype(jnp.float32) + attended
    hidden, attn_pull = jax.vjp(norm_rows, first_sum, attn_gain, attn_shift)
    hidden_low = hidden.astype(jnp.bfloat16)
    inner_act = jnp.dot(hidden_low, up_weight, preferred_element_type=jnp.float32) + up_bias
    gelu_value, gelu_pull = jax.vjp(gelu_exact, inner_act)
    active = gelu_value.astype(jnp.bfloat16)
    ffn_out = jnp.dot(active, down_weight, preferred_element_type=jnp.float32) + down_bias
    normalized_rows, ffn_pull = jax.vjp(norm_rows, hidden + ffn_out, ffn_gain, ffn_shift)
    encoded = normalized_rows.astype(jnp.bfloat16).reshape(seq_count, seq_rows, features)
    g_second, fgain_part, fshift_part = ffn_pull(
        cotangent.reshape(seq_count * seq_rows, features).astype(jnp.float32)
    )
    g_ffn = g_second.astype(jnp.bfloat16)
    dweight_part = row_dot(active, g_ffn)
    dbias_part = column_sum(g_ffn)
    (g_inner_wide,) = gelu_pull(col_dot(g_ffn, down_weight))
    g_inner = g_inner_wide.astype(jnp.bfloat16)
    uweight_part = row_dot(hidden_low, g_inner)
    ubias_part = column_sum(g_inner)
    g_hidden = g_second + col_dot(g_inner, up_weight)
    g_first, again_part, ashift_part = attn_pull(g_hidden)
    g_att = g_first.astype(jnp.bfloat16)
    oweight_part = row_dot(mixed_out, g_att)
    obias_part = column_sum(g_att)
    g_mixed = col_dot(g_att, output_weight).astype(jnp.bfloat16)
    keys_back, values_back = (
        lax.all_gather(own_keys, "blk", axis=1, tiled=True),
        lax.all_gather(own_values, "blk", axis=1, tiled=True),
    )
    key_back_heads = heads_first(keys_back)
    value_back_heads = heads_first(values_back)
    g_mixed_seq = g_mixed.reshape(seq_count, seq_rows, features)
    grad_mixed_heads = heads_first(g_mixed_seq)

    def backward_head(pieces):
        single_query_head, single_key_head, single_value_head, lse_head, head_gradient = pieces
        scores = (
            jnp.einsum(
                "pne,pme->pnm",
                single_query_head,
                single_key_head,
                preferred_element_type=jnp.float32,
            )
            * score_scale
        )
        soft_probs = jnp.where(counted, jnp.exp(scores - lse_head[..., None]), 0.0)
        reduced_probabilities = soft_probs.astype(jnp.bfloat16)
        grad_value = jnp.einsum(
            "xwr,xwa->xra", reduced_probabilities, head_gradient, preferred_element_type=jnp.float32
        )
        grad_probs = jnp.einsum(
            "pne,pme->pnm", head_gradient, single_value_head, preferred_element_type=jnp.float32
        )
        row_inner = jnp.sum(soft_probs * grad_probs, axis=-1, keepdims=True)
        score_gradient = (soft_probs * (grad_probs - row_inner)).astype(jnp.bfloat16)
        grad_query = (
            jnp.einsum(
                "ocp,opn->ocn", score_gradient, single_key_head, preferred_element_type=jnp.float32
            )
            * score_scale
        )
        grad_key = (
            jnp.einsum(
                "xwr,xwa->xra",
                score_gradient,
                single_query_head,
                preferred_element_type=jnp.float32,
            )
            * score_scale
        )
        return (grad_query, grad_key, grad_value)

    query_grads, key_grads, value_grads = lax.map(
        backward_head, (query_heads, key_back_heads, value_back_heads, lse_heads, grad_mixed_heads)
    )
    key_grads_own, value_grads_own = (
        lax.psum_scatter(
            heads_last(key_grads).astype(jnp.bfloat16), "blk", scatter_dimension=1, tiled=True
        ).astype(jnp.float32),
        lax.psum_scatter(
            heads_last(value_grads).astype(jnp.bfloat16), "blk", scatter_dimension=1, tiled=True
        ).astype(jnp.float32),
    )
    g_query = heads_last(query_grads).reshape(seq_count * seq_rows, features).astype(jnp.bfloat16)
    g_key = key_grads_own.reshape(seq_count * seq_rows, features).astype(jnp.bfloat16)
    g_value = value_grads_own.reshape(seq_count * seq_rows, features).astype(jnp.bfloat16)
    qweight_part = row_dot(flat_tokens, g_query)
    qbias_part = column_sum(g_query)
    kweight_part = row_dot(flat_tokens, g_key)
    vweight_part = row_dot(flat_tokens, g_value)
    vbias_part = column_sum(g_value)
    token_wide = (
        g_first
        + col_dot(g_query, query_weight)
        + col_dot(g_key, key_matrix)
        + col_dot(g_value, value_weight)
    )
    token_grad = token_wide.astype(jnp.bfloat16).reshape(seq_count, seq_rows, features)
    qrow, krow, vrow, orow, urow, drow = (
        lax.psum_scatter(
            qweight_part.astype(jnp.bfloat16), "dp", scatter_dimension=0, tiled=True
        ).astype(jnp.float32),
        lax.psum_scatter(
            kweight_part.astype(jnp.bfloat16), "dp", scatter_dimension=0, tiled=True
        ).astype(jnp.float32),
        lax.psum_scatter(
            vweight_part.astype(jnp.bfloat16), "dp", scatter_dimension=0, tiled=True
        ).astype(jnp.float32),
        lax.psum_scatter(
            oweight_part.astype(jnp.bfloat16), "dp", scatter_dimension=0, tiled=True
        ).astype(jnp.float32),
        lax.psum_scatter(
            uweight_part.astype(jnp.bfloat16), "dp", scatter_dimension=0, tiled=True
        ).astype(jnp.float32),
        lax.psum_scatter(
            dweight_part.astype(jnp.bfloat16), "dp", scatter_dimension=0, tiled=True
        ).astype(jnp.float32),
    )
    qfinal, kfinal, vfinal, ofinal, ufinal, dfinal = (
        lax.psum(qrow.astype(jnp.bfloat16), "blk").astype(jnp.float32),
        lax.psum(krow.astype(jnp.bfloat16), "blk").astype(jnp.float32),
        lax.psum(vrow.astype(jnp.bfloat16), "blk").astype(jnp.float32),
        lax.psum(orow.astype(jnp.bfloat16), "blk").astype(jnp.float32),
        lax.psum(urow.astype(jnp.bfloat16), "blk").astype(jnp.float32),
        lax.psum(drow.astype(jnp.bfloat16), "blk").astype(jnp.float32),
    )
    (
        qbias_sum,
        vbias_sum,
        obias_sum,
        again_sum,
        ashift_sum,
        ubias_sum,
        dbias_sum,
        fgain_sum,
        fshift_sum,
    ) = lax.psum(
        (
            qbias_part,
            vbias_part,
            obias_part,
            again_part,
            ashift_part,
            ubias_part,
            dbias_part,
            fgain_part,
            fshift_part,
        ),
        ("dp", "blk"),
    )
    return (
        encoded,
        token_grad,
        qfinal,
        qbias_sum,
        kfinal,
        vfinal,
        vbias_sum,
        ofinal,
        obias_sum,
        again_sum,
        ashift_sum,
        ufinal,
        ubias_sum,
        dfinal,
        dbias_sum,
        fgain_sum,
        fshift_sum,
    )


def solution(mesh):
    return jax.shard_map(
        on_device_fused if dict(mesh.shape) == {"dp": 16, "blk": 2} else on_device,
        mesh=mesh,
        in_specs=(
            P("dp", "blk", None),
            P("dp"),
            P("dp", "blk", None),
            P(),
            P(),
            P(),
            P(),
            P(),
            P(),
            P(),
            P(),
            P(),
            P(),
            P(),
            P(),
            P(),
            P(),
            P(),
        ),
        out_specs=(
            P("dp", "blk", None),
            P("dp", "blk", None),
            P("dp", None),
            P(),
            P("dp", None),
            P("dp", None),
            P(),
            P("dp", None),
            P(),
            P(),
            P(),
            P("dp", None),
            P(),
            P("dp", None),
            P(),
            P(),
            P(),
        ),
        check_vma=False,
    )
```

```python
import math

import jax
import jax.numpy as jnp
from jax import lax
from jax.experimental import pallas as pl
from jax.experimental.pallas import tpu as pltpu
from jax.sharding import PartitionSpec as P

MESH = pl.DeviceIdType.MESH
f32, bf16 = jnp.float32, jnp.bfloat16

HEADS = 12
EPSILON = 1e-05

LOG2E = math.log2(math.e)
LN2 = math.log(2.0)
AX = {"zh": (3, 1), "zl": (2, 2), "y": (1, 3), "x": (0, 4)}
BITS = ("c", "x", "y", "zl", "zh")
AXES = {"x": "x", "y": "y", "z": "zl", "h": "zh"}
ROUTES = {
    "D0": "xyhz", "D1": "zhxy", "D2": "yxzh", "D3": "yxzh", "D4": "zyxh", "D5": "xyzh",
    "U0": "xyzh", "U1": "yxhz", "U2": "zyxh", "U3": "xzyh", "U4": "xyhz", "U5": "zyxh",
    "O0": "yxzh", "O1": "yzxh", "O2": "zxyh", "Q0": "zhxy", "K0": "xyzh", "V0": "yxzh",
    "Q1": "yxhz", "K1": "zxyh", "V1": "xyzh", "Q2": "yxzh", "K2": "xyhz", "V2": "yxzh",
}
PIECES = tuple((n, 96 if n[0] in "DU" else 48, 128) for n in ROUTES)
NAMES = [p[0] for p in PIECES]
N_PIECES = len(PIECES)
ROW_O, ROW_AGAIN, ROW_ASHIFT, ROW_U, ROW_D, ROW_FGAIN, ROW_FSHIFT = 2, 3, 4, 5, 9, 10, 11
ROW_Q, ROW_V = 16, 17


def bit(dp, ax):
    return lax.rem(lax.div(dp, 1 << AX[ax][0]), 2)


def peer_of(ax):
    dp, c = lax.axis_index("dp"), lax.axis_index("blk")
    if ax == "c":
        return (dp, 1 - c)
    return (dp + (1 - 2 * bit(dp, ax)) * (1 << AX[ax][0]), c)


def dot_nn(a, b):
    return jnp.dot(a, b, preferred_element_type=f32)


def dot_nt(a, b):
    return lax.dot_general(a, b, (((1,), (1,)), ((), ())), preferred_element_type=f32)


def dot_tn(a, b):
    return lax.dot_general(a, b, (((0,), (0,)), ((), ())), preferred_element_type=f32)


def fold8(v):
    return jnp.sum(v.reshape(v.shape[0] // 8, 8, v.shape[1]), axis=0)


class Piece:
    def __init__(self, idx, own, other, recvs, fin, ssem, rsem):
        self.name, self.R, self.C = PIECES[idx]
        self.idx, self.own, self.other, self.recvs, self.fin = idx, own, other, recvs, fin
        self.ssem, self.rsem = ssem, rsem
        self.order = [AXES[a] for a in ROUTES[self.name]]
        self.dp = lax.axis_index("dp")
        self.gone = set()

    def view(self, k, mine):
        idx = [slice(None)] * 4
        for j in range(k):
            ax = self.order[j]
            own = bit(self.dp, ax)
            idx[AX[ax][1] - 1] = own if (j < k - 1 or mine) else 1 - own
        return tuple(idx)

    def copy(self, k):
        if k == 0:
            src, ax = self.other, "c"
        else:
            src, ax = self.own.at[self.view(k, False)], self.order[k - 1]
        return pltpu.make_async_remote_copy(
            src, self.recvs[k], self.ssem.at[self.idx], self.rsem.at[self.idx, k], device_id=peer_of(ax), device_id_type=MESH
        )

    def start(self):
        self.copy(0).start()

    def sent(self, k):
        if k not in self.gone:
            self.copy(k).wait_send()
            self.gone.add(k)

    def finish(self, k):
        self.copy(k).wait_recv()
        self.sent(k)
        v = self.view(k, True)
        total = self.own[v].astype(f32) + self.recvs[k][...].astype(f32)
        if k < 4:
            self.own[v] = total.astype(bf16)
            self.copy(k + 1).start()
        else:
            self.fin[...] = total


class Vector:
    def __init__(self, idx, acc, recv, ssem, rsem):
        self.idx, self.acc, self.recv, self.ssem, self.rsem = idx, acc, recv, ssem, rsem

    def copy(self, k):
        return pltpu.make_async_remote_copy(
            self.acc.at[k], self.recv.at[k], self.ssem.at[self.idx], self.rsem.at[self.idx, k],
            device_id=peer_of(BITS[k]), device_id_type=MESH,
        )

    def start(self, k):
        self.copy(k).start()

    def step(self, k):
        self.copy(k).wait()
        self.acc[k + 1] = self.acc[k] + self.recv[k]
        if k < 4:
            self.start(k + 1)


def layer_kernel(*refs):
    (tok_h, len_s, cot_h, wq_h, bq, wk_h, wv_h, bv, wo_h, bo, g1, b1, wu_h, bu, wd_h, bd, g2, b2) = refs[:18]
    enc_o, tg_o, du_o, small_o, vec_o, e_hbm = refs[18:24]
    (X, WU, WD, WO, Q, KO, KP, VO, VP, MB, MIX, LINV, T1, T2, T3, RSTD, HL, G, DO, CD, FAB, KR, VR,
     DU, SB, RDU, RS, SDU, SS, FDU, FS, b_acc, b_recv, l_acc, l_recv,
     VEC, LEN, wsem, vsem, esem, osem, ksem_s, ksem_r, ssem, rsem, fsem_s, fsem_r) = refs[24:]
    c = lax.axis_index("blk")
    rows = X.shape[0]
    D = X.shape[1]
    scale = 1.0 / math.sqrt(D // HEADS)

    def load(src, dst, sem):
        cp = pltpu.make_async_copy(src, dst, sem)
        cp.start()
        return cp

    ld_x = load(tok_h.at[0], X, wsem.at[5])
    ld_k = load(wk_h, WU.at[:, pl.ds(0, D)], wsem.at[0])
    vec_in = (bq, bv, bo, g1, b1, bd, g2, b2, bu)
    ld_vec = [load(v, dst, vsem.at[i]) for i, (v, dst) in enumerate(zip(vec_in, VEC))]
    ld_len = load(len_s, LEN, vsem.at[9])
    ld_v = load(wv_h, WU.at[:, pl.ds(D, D)], wsem.at[1])
    ld_q = load(wq_h, WU.at[:, pl.ds(2 * D, D)], wsem.at[2])

    barrier = pltpu.get_barrier_semaphore()
    for ax in BITS:
        pl.semaphore_signal(barrier, inc=1, device_id=peer_of(ax), device_id_type=MESH)

    def pick(half, mine, theirs):
        return jnp.where(half == c, mine, theirs)

    pieces = {}
    for i, name in enumerate(NAMES):
        if i < 12:
            own, other, recvs, fin = DU.at[i], DU.at[12 + i % 6], [r.at[i] for r in (RDU,) + SDU], du_o.at[i, c]
        else:
            k = i - 12
            own, other, recvs, fin = SB.at[k], SB.at[12 + k % 3], [r.at[k] for r in (RS,) + SS], small_o.at[k, c]
        pieces[name] = Piece(i, own, other, recvs, fin, ssem, rsem)

    def step(label):
        for name, k in HOOKS.get(label, ()):
            if name == "early":
                early.step(k)
            elif name == "late":
                late.step(k)
            else:
                pieces[name].finish(k)
                if k == 4:
                    group = min(NAMES.index(name) // 6, 2)
                    left[group] -= 1
                    if not left[group]:
                        last_copy(group).start()

    left = [6, 6, 12]

    def last_copy(g):
        src = (du_o.at[pl.ds(0, 6), c], du_o.at[pl.ds(6, 6), c], small_o.at[:, c])[g]
        dst = (FDU.at[pl.ds(0, 6)], FDU.at[pl.ds(6, 6)], FS)[g]
        return pltpu.make_async_remote_copy(
            src, dst, fsem_s.at[g], fsem_r.at[g], device_id=peer_of("c"), device_id_type=MESH
        )

    early = Vector(N_PIECES, b_acc, b_recv, ssem, rsem)
    late = Vector(N_PIECES + 1, l_acc, l_recv, ssem, rsem)
    b_acc[0] = jnp.zeros(b_acc.shape[1:], f32)

    lane = lax.broadcasted_iota(jnp.int32, (rows, 128), 1)
    low = lane < 64
    ld_len.wait()
    length = LEN[0]
    pos = lax.broadcasted_iota(jnp.int32, (rows, 128), 0)
    MB[0] = jnp.where(pos + c * rows < length, 0.0, -1e30).astype(bf16)
    MB[1] = jnp.where(pos + (1 - c) * rows < length, 0.0, -1e30).astype(bf16)

    def kv_send(src, dst, i):
        cp = pltpu.make_async_remote_copy(
            src.at[:, pl.ds(384 * (i % 2), 384)], dst.at[:, pl.ds(384 * (i % 2), 384)], ksem_s.at[6 + i], ksem_r.at[6 + i],
            device_id=peer_of("c"), device_id_type=MESH,
        )
        cp.start()
        return cp

    ld_x.wait()
    ld_k.wait()
    KO[...] = dot_nn(X[...], WU[:, :D]).astype(bf16)
    pl.semaphore_wait(barrier, 5)
    kv = [kv_send(KO, KP, 0)]
    ld_o = load(wo_h, WO, wsem.at[4])
    ld_c = load(cot_h.at[0], CD, wsem.at[6])
    for cp in ld_vec:
        cp.wait()
    bq, bv, bo, g1, b1, bd, g2, b2, bu = (v[...].reshape(1, -1) for v in VEC)
    ld_v.wait()
    VO[...] = (dot_nn(X[...], WU[:, D : 2 * D]) + bv).astype(bf16)
    kv += [kv_send(VO, VP, 2), kv_send(KO, KP, 1), kv_send(VO, VP, 3)]
    FFC = 512
    ld_q.wait()
    Q[...] = ((dot_nn(X[...], WU[:, 2 * D : 3 * D]) + bq) * (scale * LOG2E)).astype(bf16)
    ld_u = load(wu_h, WU, wsem.at[3])
    ld_d = load(wd_h, WD, wsem.at[1])

    one, zero = jnp.ones((rows, 128), bf16), jnp.zeros((rows, 128), bf16)
    hot = [jnp.where(lane == 64, 1.0, 0.0).astype(bf16), jnp.where(lane == 0, 1.0, 0.0).astype(bf16)]

    def own_lanes(j, mine, rest):
        return jnp.where(low, mine, rest) if j == 0 else jnp.where(low, rest, mine)

    def e_slot(row, h, n, sem, out):
        buf, far = FAB.at[pl.ds(row, 1024 * n), :], e_hbm.at[pl.ds(1024 * h, 1024 * n), :]
        return pltpu.make_async_copy(buf, far, sem) if out else pltpu.make_async_copy(far, buf, sem)

    def e_out(g):
        return e_slot(3072 * (g % 2), 3 * g, 3, esem.at[g % 2], True)

    res = []
    for h in range(HEADS):
        p, j = divmod(h, 2)
        g = h // 3
        ls = slice(128 * p, 128 * p + 128)
        if h == 0:
            kv[0].wait_recv()
            kv[1].wait_recv()
        if h == 6:
            kv[2].wait_recv()
            kv[3].wait_recv()
        if h % 3 == 0 and g >= 2:
            e_out(g - 2).wait()
        q = own_lanes(j, Q[:, ls], hot[j])
        s_o = dot_nt(q, own_lanes(j, KO[:, ls], MB[0]))
        s_p = dot_nt(q, own_lanes(j, KP[:, ls], MB[1]))
        m = jnp.maximum(jnp.max(s_o, axis=1, keepdims=True), jnp.max(s_p, axis=1, keepdims=True))
        e_o = jnp.exp2(s_o - m).astype(bf16)
        e_p = jnp.exp2(s_p - m).astype(bf16)
        base = 1024 * (h % 6)
        FAB[base : base + 512, :] = e_o
        FAB[base + 512 : base + 1024, :] = e_p
        res.append(dot_nn(e_o, own_lanes(j, VO[:, ls], one)) + dot_nn(e_p, own_lanes(j, VP[:, ls], one)))
        if j == 1:
            inv = 1.0 / pltpu.roll(jnp.where(low, res[1], res[0]), 64, 1)
            MIX[:, ls] = (jnp.where(low, res[0], res[1]) * inv).astype(bf16)
            LINV[:, ls] = inv
            res = []
        if h % 3 == 2:
            e_out(g).start()

    ld_o.wait()
    T2[...] = dot_nn(MIX[...], WO[...])
    BR = 128
    for r in range(0, rows, BR):
        rs = slice(r, r + BR)
        r1 = X[rs, :].astype(f32) + (T2[rs, :] + bo)
        cen = r1 - jnp.mean(r1, axis=1, keepdims=True)
        rstd = lax.rsqrt(jnp.mean(cen * cen, axis=1, keepdims=True) + EPSILON)
        xh = cen * rstd
        T1[rs, :] = xh
        RSTD[rs, :] = rstd
        HL[rs, :] = (xh * g1 + b1).astype(bf16)
    e_out(2).wait()
    e_out(3).wait()

    ld_u.wait()
    ld_d.wait()
    for j in range(6):
        u = dot_nn(HL[...], WU[:, FFC * j : FFC * j + FFC]) + bu[:, FFC * j : FFC * j + FFC]
        half = 0.5 * (1.0 + lax.erf(u * (1.0 / math.sqrt(2.0))))
        act = (u * half).astype(bf16)
        FAB[512 * j : 512 * j + 512, :] = act
        slope = half + u * (jnp.exp(u * u * -0.5) * (1.0 / math.sqrt(2.0 * math.pi)))
        FAB[3072 + 512 * j : 3072 + 512 * j + 512, :] = slope.astype(bf16)
        y = dot_nn(act, WD[FFC * j : FFC * j + FFC, :])
        T2[...] = y if j == 0 else T2[...] + y

    ld_c.wait()
    sums = [jnp.zeros((8, D), f32)] * 3
    for r in range(0, rows, BR):
        rs = slice(r, r + BR)
        r2 = (T1[rs, :] * g1 + b1) + (T2[rs, :] + bd)
        cen = r2 - jnp.mean(r2, axis=1, keepdims=True)
        rstd = lax.rsqrt(jnp.mean(cen * cen, axis=1, keepdims=True) + EPSILON)
        xh = cen * rstd
        DO[rs, :] = (xh * g2 + b2).astype(bf16)
        dy = CD[rs, :].astype(f32)
        dx = dy * g2
        g = rstd * (dx - jnp.mean(dx, axis=1, keepdims=True) - xh * jnp.mean(dx * xh, axis=1, keepdims=True))
        T2[rs, :] = g
        gl = g.astype(bf16)
        G[rs, :] = gl
        sums = [sums[0] + fold8(dy * xh), sums[1] + fold8(dy), sums[2] + fold8(gl.astype(f32))]
    enc_copy = load(DO, enc_o.at[0], osem.at[0])
    for row, s in zip((ROW_FGAIN, ROW_FSHIFT, ROW_D), sums):
        b_acc[0, row : row + 1, :] = jnp.sum(s, axis=0, keepdims=True)

    for t in range(3):
        for j in range(6):
            w = dot_tn(FAB[512 * j : 512 * j + 512, :], G[:, 256 * t : 256 * t + 256]).astype(bf16)
            at = 512 * j
            while at < 512 * j + 512:
                seg, off = divmod(at, 96)
                size = min(96 - off, 512 * j + 512 - at)
                i, half = divmod(seg, 2)
                for u in range(2):
                    where = (pick(half, 2 * t + u, 12 + 2 * t + u), i // 8, (i // 4) % 2, (i // 2) % 2, i % 2)
                    DU[where + (slice(off, off + size),)] = w[at - 512 * j : at - 512 * j + size, 128 * u : 128 * u + 128]
                at += size
        pieces["D%d" % (2 * t)].start()
        pieces["D%d" % (2 * t + 1)].start()
        step("D%d" % t)

    def e_in(h):
        slot = h % 4
        return e_slot((0, 1024, 2048, 6144)[slot], h, 1, esem.at[slot], False)

    for h in range(4):
        e_in(h).start()

    for n, j in enumerate((0, 3, 1, 4, 2, 5)):
        hf, t = divmod(j, 3)
        frow = slice(3072 + 512 * j, 3072 + 512 * j + 512)
        gi32 = dot_nt(G[...], WD[FFC * j : FFC * j + FFC, :]) * FAB[frow, :].astype(f32)
        gi = gi32.astype(bf16)
        step("G%d" % n)
        FAB[frow, :] = gi
        s = jnp.sum(fold8(gi.astype(f32)), axis=0, keepdims=True)
        at = 512 * j
        while at < 512 * j + 512:
            row, off = divmod(at, D)
            size = min(D - off, 512 * j + 512 - at)
            b_acc[0, ROW_U + row : ROW_U + row + 1, off : off + size] = s[:, at - 512 * j : at - 512 * j + size]
            at += size
        w = dot_tn(HL[...], gi).astype(bf16)
        if hf == 0:
            pieces["D%d" % (2 * t)].sent(0)
            pieces["D%d" % (2 * t + 1)].sent(0)
        for u in range(2):
            dst = pick(hf, 6 + 2 * t + u, 12 + 2 * t + u)
            for i in range(16):
                where = (dst, i // 8, (i // 4) % 2, (i // 2) % 2, i % 2)
                for v in range(2):
                    col = 256 * u + 128 * v
                    DU[where + (slice(48 * v, 48 * v + 48),)] = w[48 * i : 48 * i + 48, col : col + 128]
        y = dot_nt(gi, WU[:, FFC * j : FFC * j + FFC])
        T3[...] = (T2[...] if n == 0 else T3[...]) + y
        if hf == 1:
            pieces["U%d" % (2 * t)].start()
            pieces["U%d" % (2 * t + 1)].start()
        step("F%d" % n)

    ld_q = load(wq_h, WU.at[:, pl.ds(0, D)], wsem.at[0])
    ld_k = load(wk_h, WU.at[:, pl.ds(D, D)], wsem.at[1])
    ld_v = load(wv_h, WU.at[:, pl.ds(2 * D, D)], wsem.at[2])

    sums = [jnp.zeros((8, D), f32)] * 3
    for r in range(0, rows, BR):
        rs = slice(r, r + BR)
        gh = T3[rs, :]
        xh = T1[rs, :]
        dx = gh * g1
        g = RSTD[rs, :] * (dx - jnp.mean(dx, axis=1, keepdims=True) - xh * jnp.mean(dx * xh, axis=1, keepdims=True))
        T3[rs, :] = g
        gl = g.astype(bf16)
        G[rs, :] = gl
        sums = [sums[0] + fold8(gh * xh), sums[1] + fold8(gh), sums[2] + fold8(gl.astype(f32))]
    for row, s in zip((ROW_AGAIN, ROW_ASHIFT, ROW_O), sums):
        b_acc[0, row : row + 1, :] = jnp.sum(s, axis=0, keepdims=True)
    early.start(0)
    step("N")

    w = dot_tn(MIX[...], G[...]).astype(bf16)
    for half in range(2):
        for t in range(3):
            at = 384 * half + 128 * t
            SB[pick(half, t, 12 + t)] = w[:, at : at + 128].reshape(2, 2, 2, 2, 48, 128)
    for t in range(3):
        pieces["O%d" % t].start()
    step("M")
    enc_copy.wait()
    DO[...] = dot_nt(G[...], WO[...]).astype(bf16)

    step("P")

    def projection(m, t, grad):
        pieces[NAMES[12 + 3 * t + m]].sent(0)
        w = dot_tn(X[...], grad).astype(bf16)
        for half in range(2):
            SB[pick(half, 3 + 3 * t + m, 12 + m)] = w[:, 128 * half : 128 * half + 128].reshape(2, 2, 2, 2, 48, 128)

    def key_value(t):
        cs = slice(256 * t, 256 * t + 256)
        HL[:, cs] = (FAB[KT + 256 * t : KT + 256 * t + 256, :].astype(f32) + KR[cs, :].astype(f32)).astype(bf16).T
        projection(1, t, HL[:, cs])
        G[:, cs] = (FAB[VT + 256 * t : VT + 256 * t + 256, :].astype(f32) + VR[cs, :].astype(f32)).astype(bf16).T
        projection(2, t, G[:, cs])

    KT, KTP, VT, VTP = 3072, 3072 + D, 3072 + 2 * D, 3072 + 3 * D
    back = []
    for p in range(HEADS // 2):
        ls = slice(128 * p, 128 * p + 128)
        ps = 128 * p
        dos = DO[:, ls].astype(f32) * LINV[:, ls]
        extra = pltpu.roll(dos * MIX[:, ls].astype(f32), 64, 1) * -1.0
        dos = dos.astype(bf16)
        extra = extra.astype(bf16)
        dos_t = dos.T
        q_t = Q[:, ls].T
        dq = []
        e_in(2 * p).wait()
        e_in(2 * p + 1).wait()
        t = p // 2
        if p in (3, 5):
            back[2 * t - 2].wait_recv()
            back[2 * t - 1].wait_recv()
        for j in range(2):
            h = 2 * p + j
            base = (0, 1024, 2048, 6144)[h % 4]
            d_ext = own_lanes(j, dos, extra)
            rt = slice(64 * j, 64 * j + 64)
            acc = None
            for half, (k, v, kt, vt) in enumerate(((KO, VO, KT, VT), (KP, VP, KTP, VTP))):
                e = FAB[base + 512 * half : base + 512 * half + 512, :]
                dp = dot_nt(d_ext, own_lanes(j, v[:, ls], one))
                ds = (e.astype(f32) * dp).astype(bf16)
                x = dot_nn(ds, k[:, ls])
                acc = x if acc is None else acc + x
                FAB[vt + ps + 64 * j : vt + ps + 64 * j + 64, :] = dot_nn(dos_t[rt], e).astype(bf16)
                FAB[kt + ps + 64 * j : kt + ps + 64 * j + 64, :] = (dot_nn(q_t[rt], ds) * LN2).astype(bf16)
            dq.append(acc)
        CD[:, ls] = (jnp.where(low, dq[0], dq[1]) * scale).astype(bf16)
        if p % 2 == 1:
            projection(0, t, CD[:, 256 * t : 256 * t + 256])
        if p in (3, 5):
            key_value(t - 1)
        if p + 2 < HEADS // 2:
            e_in(2 * p + 4).start()
            e_in(2 * p + 5).start()
        if p % 2 == 1:
            for i, (src, dst) in enumerate(((KTP, KR), (VTP, VR))):
                cp = pltpu.make_async_remote_copy(
                    FAB.at[pl.ds(src + 256 * t, 256), :], dst.at[pl.ds(256 * t, 256), :],
                    ksem_s.at[2 * t + i], ksem_r.at[2 * t + i], device_id=peer_of("c"), device_id_type=MESH,
                )
                cp.start()
                back.append(cp)
            pieces["Q%d" % t].start()
        if p in (3, 5):
            pieces["K%d" % (t - 1)].start()
            pieces["V%d" % (t - 1)].start()
        step("H%d" % p)

    ld_q.wait()
    ld_k.wait()
    ld_v.wait()
    T3[...] += dot_nt(CD[...], WU[:, :D])
    late.acc[0, 0:1, :] = jnp.sum(fold8(CD[...].astype(f32)), axis=0, keepdims=True)
    late.acc[0, 2:8, :] = jnp.zeros((6, D), f32)
    back[4].wait_recv()
    back[5].wait_recv()
    key_value(2)
    late.acc[0, 1:2, :] = jnp.sum(fold8(G[...].astype(f32)), axis=0, keepdims=True)
    pieces["K2"].start()
    pieces["V2"].start()
    late.start(0)
    step("V")
    MIX[...] = (T3[...] + dot_nt(HL[...], WU[:, D : 2 * D]) + dot_nt(G[...], WU[:, 2 * D : 3 * D])).astype(bf16)
    tg_copy = load(MIX, tg_o.at[0], osem.at[1])

    step("T")
    vec_o[0:16, :] = early.acc[5]
    vec_o[16:24, :] = late.acc[5]

    outs = []
    for g in range(3):
        last_copy(g).wait_recv()
    du_o[:, 1 - c] = FDU[...]
    small_o[:, 1 - c] = FS[...]
    tg_copy.wait()
    for cp in kv + back:
        cp.wait_send()
    for g in range(3):
        last_copy(g).wait_send()


HOOKS = {
    "D2": (("D0", 0), ("D1", 0),),
    "G0": (("D2", 0), ("D3", 0), ("D4", 0), ("D5", 0),),
    "F3": (("U0", 0), ("U1", 0), ("D0", 1),),
    "F4": (("D1", 1), ("U2", 0), ("U3", 0), ("D5", 1), ("D4", 1),),
    "F5": (("D2", 1), ("D3", 1),),
    "M": (("U4", 0), ("U5", 0),),
    "P": (("early", 0),),
    "H0": (("O0", 0), ("O1", 0), ("O2", 0), ("D1", 2), ("U0", 1), ("D0", 2),),
    "H1": (("D5", 2), ("D4", 2), ("U2", 1),),
    "H2": (("Q0", 0),),
    "H3": (("early", 1), ("U1", 1), ("D0", 3), ("D2", 2), ("D3", 2), ("D1", 3), ("D5", 3), ("O2", 1),),
    "H4": (("U5", 1), ("D4", 3), ("K0", 0), ("Q1", 0), ("V0", 0), ("U3", 1), ("O0", 1), ("O1", 1), ("U0", 2),
        ("Q0", 1),),
    "H5": (("U2", 2), ("D1", 4), ("D0", 4), ("early", 2), ("U4", 1), ("D5", 4), ("O2", 2), ("D2", 3), ("D3", 3),),
    "V": (("D4", 4), ("U1", 2), ("K1", 0), ("Q2", 0), ("V1", 0), ("O0", 2),),
    "T": (("K0", 1), ("late", 0), ("U2", 3), ("K2", 0), ("V2", 0), ("O1", 2), ("U0", 3), ("Q0", 2), ("U5", 2),
        ("O2", 3), ("D2", 4), ("D3", 4), ("Q1", 1), ("V0", 1), ("O0", 3), ("early", 3), ("late", 1), ("O2", 4),
        ("V1", 1), ("O1", 3), ("U3", 2), ("Q0", 3), ("U2", 4), ("K0", 2), ("U0", 4), ("U1", 3), ("U4", 2), ("O0", 4),
        ("Q2", 1), ("U5", 3), ("K1", 1), ("Q1", 2), ("V0", 2), ("late", 2), ("O1", 4), ("Q0", 4), ("K2", 1),
        ("V2", 1), ("early", 4), ("K0", 3), ("U1", 4), ("V1", 2), ("U3", 3), ("Q2", 2), ("K1", 2), ("K2", 2),
        ("V2", 2), ("U5", 4), ("V0", 3), ("late", 3), ("U4", 3), ("Q1", 3), ("K0", 4), ("K1", 3), ("V1", 3),
        ("U3", 4), ("Q2", 3), ("K2", 3), ("V2", 3), ("V0", 4), ("Q1", 4), ("K1", 4), ("U4", 4), ("late", 4),
        ("V1", 4), ("Q2", 4), ("K2", 4), ("V2", 4),),
}


def layer_call(tokens, lengths, cotangent, wq, bq, wk, wv, bv, wo, bo, g1, b1, wu, bu, wd, bd, g2, b2):
    rows, D = tokens.shape[1:]
    lead = (2, 2, 2, 2)

    def ladder(n, R, C):
        return tuple(pltpu.VMEM((n,) + (2,) * (4 - k) + (R, C), bf16) for k in range(1, 5))

    big = pltpu.VMEM((rows, D), f32)
    low = pltpu.VMEM((rows, D), bf16)
    wide = pltpu.VMEM((D, D), bf16)
    scratch = [
        low, pltpu.VMEM((D, 4 * D), bf16), pltpu.VMEM((4 * D, D), bf16), wide, low, low, low, low, low, pltpu.VMEM((2, rows, 128), bf16), low, big,
        big, big, big, pltpu.VMEM((rows, 1), f32), low, low, low, low, pltpu.VMEM((7168, 512), bf16),
        pltpu.VMEM((D, rows), bf16), pltpu.VMEM((D, rows), bf16),
        pltpu.VMEM((18,) + lead + (96, 128), bf16), pltpu.VMEM((15,) + lead + (48, 128), bf16),
        pltpu.VMEM((12,) + lead + (96, 128), bf16), pltpu.VMEM((12,) + lead + (48, 128), bf16),
        ladder(12, 96, 128), ladder(12, 48, 128),
        pltpu.VMEM((12, 96, 128), f32), pltpu.VMEM((12, 48, 128), f32),
        pltpu.VMEM((6, 16, D), f32), pltpu.VMEM((5, 16, D), f32), pltpu.VMEM((6, 8, D), f32), pltpu.VMEM((5, 8, D), f32),
        (pltpu.VMEM((D,), f32),) * 8 + (pltpu.VMEM((4 * D,), f32),), pltpu.SMEM((1,), jnp.int32),
        pltpu.SemaphoreType.DMA((7,)), pltpu.SemaphoreType.DMA((10,)), pltpu.SemaphoreType.DMA((4,)),
        pltpu.SemaphoreType.DMA((6,)), pltpu.SemaphoreType.DMA((10,)), pltpu.SemaphoreType.DMA((10,)),
        pltpu.SemaphoreType.DMA((N_PIECES + 2,)), pltpu.SemaphoreType.DMA((N_PIECES + 2, 5)),
        pltpu.SemaphoreType.DMA((3,)), pltpu.SemaphoreType.DMA((3,)),
    ]
    hbm = pl.BlockSpec(memory_space=pl.ANY)
    vm = pl.BlockSpec(memory_space=pltpu.VMEM)
    sds = jax.ShapeDtypeStruct
    shapes = [sds(tokens.shape, bf16), sds(tokens.shape, bf16), pltpu.VMEM((12, 2, 96, 128), f32), pltpu.VMEM((12, 2, 48, 128), f32),
              pltpu.VMEM((24, D), f32), sds((HEADS * 1024, 512), bf16)]
    return pl.pallas_call(
        layer_kernel,
        out_shape=shapes,
        in_specs=[hbm] * 18,
        out_specs=[hbm, hbm, vm, vm, vm, hbm],
        scratch_shapes=scratch,
        compiler_params=pltpu.CompilerParams(collective_id=0, has_side_effects=True, vmem_limit_bytes=VMEM_LIMIT),
    )(tokens, lengths, cotangent, wq, bq, wk, wv, bv, wo, bo, g1, b1, wu, bu, wd, bd,
      g2, b2)


VMEM_LIMIT = 62 << 20


def hand_on_kernel(enc, tg, du, small, vec, *refs):
    outs, vecs = refs[:8], refs[8 : 8 + len(VEC_ROWS)]
    stage, done, sem = refs[8 + len(VEC_ROWS) : -7], refs[-7:-1], refs[-1]
    ins = [pltpu.make_async_copy(r, s, sem.at[i]) for i, (r, s) in enumerate(zip((enc, tg), stage))]
    for cp in ins:
        cp.start()
    back = [pltpu.make_async_copy(s, o, sem.at[2 + i]) for i, (s, o) in enumerate(zip(stage + done, outs))]
    q, k, v, o, u, d = done
    for t in range(6):
        for half in range(2):
            d[96 * half : 96 * half + 96, 128 * t : 128 * t + 128] = du[t, half]
            for w in range(2):
                col = 1536 * half + 256 * t + 128 * w
                u[:, col : col + 128] = du[6 + t, half, 48 * w : 48 * w + 48]
    back[7].start()
    back[6].start()
    for t in range(3):
        for half in range(2):
            o[:, 384 * half + 128 * t : 384 * half + 128 * t + 128] = small[t, half]
            for m, w in enumerate((q, k, v)):
                w[:, 128 * half + 256 * t : 128 * half + 256 * t + 128] = small[3 + 3 * t + m, half]
    for i in range(2, 6):
        back[i].start()
    for i in range(2):
        ins[i].wait()
        back[i].start()
    for ref, (row, count) in zip(vecs, VEC_ROWS):
        for k in range(count):
            ref[768 * k : 768 * k + 768] = vec[row + k]
    for cp in back:
        cp.wait()


VEC_ROWS = ((ROW_Q, 1), (ROW_V, 1), (ROW_O, 1), (ROW_AGAIN, 1), (ROW_ASHIFT, 1), (ROW_U, 4), (ROW_D, 1), (ROW_FGAIN, 1),
            (ROW_FSHIFT, 1))


def hand_on(arrays):
    hbm = pl.BlockSpec(memory_space=pl.ANY)
    vm = pl.BlockSpec(memory_space=pltpu.VMEM)
    shapes = [(a.shape, a.dtype) for a in arrays[:2]] + [((48, 768), f32)] * 4 + [((48, 3072), f32), ((192, 768), f32)]
    return pl.pallas_call(
        hand_on_kernel,
        out_shape=[jax.ShapeDtypeStruct(*a) for a in shapes] + [jax.ShapeDtypeStruct((768 * k,), f32) for _, k in VEC_ROWS],
        in_specs=[pl.BlockSpec(memory_space=pltpu.HBM)] * 2 + [vm] * 3,
        out_specs=[hbm] * 8 + [vm] * len(VEC_ROWS),
        scratch_shapes=[pltpu.VMEM(a.shape, a.dtype) for a in arrays[:2]] + [pltpu.VMEM(*a) for a in shapes[2:]]
        + [pltpu.SemaphoreType.DMA((10,))],
        compiler_params=pltpu.CompilerParams(vmem_limit_bytes=32 << 20),
    )(*arrays)


def on_device_fused(*args):
    (enc, tg, qg, kg, vg, og, ug, dg, qb, vb, ob, ag, ash, ub, db, fg, fs) = hand_on(layer_call(*args)[:5])
    return (enc, tg, qg, qb, kg, vg, vb, og, ob, ag, ash, ug, ub, dg, db, fg, fs)


CONTRACT_ROWS = (((0,), (0,)), ((), ()))
CONTRACT_COLS = (((1,), (1,)), ((), ()))


def norm_rows(values_in, gain_vec, shift_vec):
    row_mean = jnp.mean(values_in, axis=-1, keepdims=True)
    centred = values_in - row_mean
    spread = jnp.mean(centred * centred, axis=-1, keepdims=True)
    return centred * lax.rsqrt(spread + EPSILON) * gain_vec + shift_vec


def gelu_exact(values_in):
    return 0.5 * values_in * (1.0 + lax.erf(values_in * (1.0 / math.sqrt(2.0))))


def row_dot(left, right):
    return lax.dot_general(left, right, CONTRACT_ROWS, preferred_element_type=jnp.float32)


def col_dot(left, right):
    return lax.dot_general(left, right, CONTRACT_COLS, preferred_element_type=jnp.float32)


def heads_first(values_in):
    seq_count, positions, features = values_in.shape
    return jnp.moveaxis(values_in.reshape(seq_count, positions, HEADS, features // HEADS), 2, 0)


def heads_last(values_in):
    head_count, seq_count, positions, head_size = values_in.shape
    return jnp.moveaxis(values_in, 0, 2).reshape(seq_count, positions, head_count * head_size)


def column_sum(values_in):
    return jnp.sum(values_in.astype(jnp.float32), axis=0)


def on_device(
    tokens,
    lengths,
    cotangent,
    query_weight,
    query_bias,
    key_matrix,
    value_weight,
    value_bias,
    output_weight,
    output_bias,
    attn_gain,
    attn_shift,
    up_weight,
    up_bias,
    down_weight,
    down_bias,
    ffn_gain,
    ffn_shift,
):
    seq_count, seq_rows, features = tokens.shape
    key_total = seq_rows * lax.axis_size("blk")
    score_scale = 1.0 / math.sqrt(features // HEADS)
    flat_tokens = tokens.reshape(seq_count * seq_rows, features)
    counted = jnp.arange(key_total, dtype=jnp.int32)[None, None, :] < lengths[:, None, None]
    queries = (
        jnp.dot(flat_tokens, query_weight, preferred_element_type=jnp.float32) + query_bias
    ).astype(jnp.bfloat16)
    keyset = jnp.dot(flat_tokens, key_matrix, preferred_element_type=jnp.float32).astype(
        jnp.bfloat16
    )
    valset = (
        jnp.dot(flat_tokens, value_weight, preferred_element_type=jnp.float32) + value_bias
    ).astype(jnp.bfloat16)
    own_keys = keyset.reshape(seq_count, seq_rows, features)
    own_values = valset.reshape(seq_count, seq_rows, features)
    keys_all, values_all = (
        lax.all_gather(own_keys, "blk", axis=1, tiled=True),
        lax.all_gather(own_values, "blk", axis=1, tiled=True),
    )
    query_seq = queries.reshape(seq_count, seq_rows, features)
    query_heads = heads_first(query_seq)
    key_heads = heads_first(keys_all)
    value_heads = heads_first(values_all)

    def forward_head(pieces):
        single_query_head, single_key_head, single_value_head = pieces
        scores = (
            jnp.einsum(
                "pne,pme->pnm",
                single_query_head,
                single_key_head,
                preferred_element_type=jnp.float32,
            )
            * score_scale
        )
        masked = jnp.where(counted, scores, -1e30)
        largest = jnp.max(masked, axis=-1, keepdims=True)
        raised = jnp.exp(masked - largest)
        row_total = jnp.sum(raised, axis=-1, keepdims=True)
        reduced_probabilities = (raised / row_total).astype(jnp.bfloat16)
        mixed_head = jnp.einsum(
            "ocp,opn->ocn",
            reduced_probabilities,
            single_value_head,
            preferred_element_type=jnp.float32,
        )
        return (mixed_head.astype(jnp.bfloat16), (largest + jnp.log(row_total))[..., 0])

    mixed_heads, lse_heads = lax.map(forward_head, (query_heads, key_heads, value_heads))
    mixed_out = heads_last(mixed_heads).reshape(seq_count * seq_rows, features)
    attended = jnp.dot(mixed_out, output_weight, preferred_element_type=jnp.float32) + output_bias
    first_sum = flat_tokens.astype(jnp.float32) + attended
    hidden, attn_pull = jax.vjp(norm_rows, first_sum, attn_gain, attn_shift)
    hidden_low = hidden.astype(jnp.bfloat16)
    inner_act = jnp.dot(hidden_low, up_weight, preferred_element_type=jnp.float32) + up_bias
    gelu_value, gelu_pull = jax.vjp(gelu_exact, inner_act)
    active = gelu_value.astype(jnp.bfloat16)
    ffn_out = jnp.dot(active, down_weight, preferred_element_type=jnp.float32) + down_bias
    normalized_rows, ffn_pull = jax.vjp(norm_rows, hidden + ffn_out, ffn_gain, ffn_shift)
    encoded = normalized_rows.astype(jnp.bfloat16).reshape(seq_count, seq_rows, features)
    g_second, fgain_part, fshift_part = ffn_pull(
        cotangent.reshape(seq_count * seq_rows, features).astype(jnp.float32)
    )
    g_ffn = g_second.astype(jnp.bfloat16)
    dweight_part = row_dot(active, g_ffn)
    dbias_part = column_sum(g_ffn)
    (g_inner_wide,) = gelu_pull(col_dot(g_ffn, down_weight))
    g_inner = g_inner_wide.astype(jnp.bfloat16)
    uweight_part = row_dot(hidden_low, g_inner)
    ubias_part = column_sum(g_inner)
    g_hidden = g_second + col_dot(g_inner, up_weight)
    g_first, again_part, ashift_part = attn_pull(g_hidden)
    g_att = g_first.astype(jnp.bfloat16)
    oweight_part = row_dot(mixed_out, g_att)
    obias_part = column_sum(g_att)
    g_mixed = col_dot(g_att, output_weight).astype(jnp.bfloat16)
    keys_back, values_back = (
        lax.all_gather(own_keys, "blk", axis=1, tiled=True),
        lax.all_gather(own_values, "blk", axis=1, tiled=True),
    )
    key_back_heads = heads_first(keys_back)
    value_back_heads = heads_first(values_back)
    g_mixed_seq = g_mixed.reshape(seq_count, seq_rows, features)
    grad_mixed_heads = heads_first(g_mixed_seq)

    def backward_head(pieces):
        single_query_head, single_key_head, single_value_head, lse_head, head_gradient = pieces
        scores = (
            jnp.einsum(
                "pne,pme->pnm",
                single_query_head,
                single_key_head,
                preferred_element_type=jnp.float32,
            )
            * score_scale
        )
        soft_probs = jnp.where(counted, jnp.exp(scores - lse_head[..., None]), 0.0)
        reduced_probabilities = soft_probs.astype(jnp.bfloat16)
        grad_value = jnp.einsum(
            "xwr,xwa->xra", reduced_probabilities, head_gradient, preferred_element_type=jnp.float32
        )
        grad_probs = jnp.einsum(
            "pne,pme->pnm", head_gradient, single_value_head, preferred_element_type=jnp.float32
        )
        row_inner = jnp.sum(soft_probs * grad_probs, axis=-1, keepdims=True)
        score_gradient = (soft_probs * (grad_probs - row_inner)).astype(jnp.bfloat16)
        grad_query = (
            jnp.einsum(
                "ocp,opn->ocn", score_gradient, single_key_head, preferred_element_type=jnp.float32
            )
            * score_scale
        )
        grad_key = (
            jnp.einsum(
                "xwr,xwa->xra",
                score_gradient,
                single_query_head,
                preferred_element_type=jnp.float32,
            )
            * score_scale
        )
        return (grad_query, grad_key, grad_value)

    query_grads, key_grads, value_grads = lax.map(
        backward_head, (query_heads, key_back_heads, value_back_heads, lse_heads, grad_mixed_heads)
    )
    key_grads_own, value_grads_own = (
        lax.psum_scatter(
            heads_last(key_grads).astype(jnp.bfloat16), "blk", scatter_dimension=1, tiled=True
        ).astype(jnp.float32),
        lax.psum_scatter(
            heads_last(value_grads).astype(jnp.bfloat16), "blk", scatter_dimension=1, tiled=True
        ).astype(jnp.float32),
    )
    g_query = heads_last(query_grads).reshape(seq_count * seq_rows, features).astype(jnp.bfloat16)
    g_key = key_grads_own.reshape(seq_count * seq_rows, features).astype(jnp.bfloat16)
    g_value = value_grads_own.reshape(seq_count * seq_rows, features).astype(jnp.bfloat16)
    qweight_part = row_dot(flat_tokens, g_query)
    qbias_part = column_sum(g_query)
    kweight_part = row_dot(flat_tokens, g_key)
    vweight_part = row_dot(flat_tokens, g_value)
    vbias_part = column_sum(g_value)
    token_wide = (
        g_first
        + col_dot(g_query, query_weight)
        + col_dot(g_key, key_matrix)
        + col_dot(g_value, value_weight)
    )
    token_grad = token_wide.astype(jnp.bfloat16).reshape(seq_count, seq_rows, features)
    qrow, krow, vrow, orow, urow, drow = (
        lax.psum_scatter(
            qweight_part.astype(jnp.bfloat16), "dp", scatter_dimension=0, tiled=True
        ).astype(jnp.float32),
        lax.psum_scatter(
            kweight_part.astype(jnp.bfloat16), "dp", scatter_dimension=0, tiled=True
        ).astype(jnp.float32),
        lax.psum_scatter(
            vweight_part.astype(jnp.bfloat16), "dp", scatter_dimension=0, tiled=True
        ).astype(jnp.float32),
        lax.psum_scatter(
            oweight_part.astype(jnp.bfloat16), "dp", scatter_dimension=0, tiled=True
        ).astype(jnp.float32),
        lax.psum_scatter(
            uweight_part.astype(jnp.bfloat16), "dp", scatter_dimension=0, tiled=True
        ).astype(jnp.float32),
        lax.psum_scatter(
            dweight_part.astype(jnp.bfloat16), "dp", scatter_dimension=0, tiled=True
        ).astype(jnp.float32),
    )
    qfinal, kfinal, vfinal, ofinal, ufinal, dfinal = (
        lax.psum(qrow.astype(jnp.bfloat16), "blk").astype(jnp.float32),
        lax.psum(krow.astype(jnp.bfloat16), "blk").astype(jnp.float32),
        lax.psum(vrow.astype(jnp.bfloat16), "blk").astype(jnp.float32),
        lax.psum(orow.astype(jnp.bfloat16), "blk").astype(jnp.float32),
        lax.psum(urow.astype(jnp.bfloat16), "blk").astype(jnp.float32),
        lax.psum(drow.astype(jnp.bfloat16), "blk").astype(jnp.float32),
    )
    (
        qbias_sum,
        vbias_sum,
        obias_sum,
        again_sum,
        ashift_sum,
        ubias_sum,
        dbias_sum,
        fgain_sum,
        fshift_sum,
    ) = lax.psum(
        (
            qbias_part,
            vbias_part,
            obias_part,
            again_part,
            ashift_part,
            ubias_part,
            dbias_part,
            fgain_part,
            fshift_part,
        ),
        ("dp", "blk"),
    )
    return (
        encoded,
        token_grad,
        qfinal,
        qbias_sum,
        kfinal,
        vfinal,
        vbias_sum,
        ofinal,
        obias_sum,
        again_sum,
        ashift_sum,
        ufinal,
        ubias_sum,
        dfinal,
        dbias_sum,
        fgain_sum,
        fshift_sum,
    )


def solution(mesh):
    return jax.shard_map(
        on_device_fused if dict(mesh.shape) == {"dp": 16, "blk": 2} else on_device,
        mesh=mesh,
        in_specs=(
            P("dp", "blk", None),
            P("dp"),
            P("dp", "blk", None),
            P(),
            P(),
            P(),
            P(),
            P(),
            P(),
            P(),
            P(),
            P(),
            P(),
            P(),
            P(),
            P(),
            P(),
            P(),
        ),
        out_specs=(
            P("dp", "blk", None),
            P("dp", "blk", None),
            P("dp", None),
            P(),
            P("dp", None),
            P("dp", None),
            P(),
            P("dp", None),
            P(),
            P(),
            P(),
            P("dp", None),
            P(),
            P("dp", None),
            P(),
            P(),
            P(),
        ),
        check_vma=False,
    )
```
